512 devices in a mesh: prow: 32 (over x, z), pcol: 16 (over y, core).
Axes of the slice: x: 4, y: 8, z: 8, core: 2. Of those that a mesh axis runs over, the one named last changes fastest.
Arguments:
- factor: bfloat16 [32, 1, 16, 2, 512, 512], P('prow', None, 'pcol'), may hold values from -0.125 to 0.125
- rhs: float32 [32, 1, 512, 128], P('prow'), may hold values from -6 to 6
- upper_inverse: bfloat16 [32, 1, 512, 512], P('prow')
- lower_inverse: bfloat16 [32, 1, 512, 512], P('prow')
- parents: int32 [32], replicated, may hold values from 16 to 32, as said below
- block_mask: int32 [32, 32], replicated, may hold values 0 or 1
Outputs:
- solution: float32 [32, 1, 512, 128], P('prow')
The draws below stay inside these ranges and needn't reach their ends.
Inputs may be any that keep to these rules, and one draw needn't show every extreme that they name: `parents`: the parent of a supernode of level l below the top is a supernode of level l + 1; supernodes of the top level have parent 32.
All inputs are finite; a program needn't handle non-finite values.
Results may differ from the reference program's by a relative error of at most 0.0003.
Values sent between devices are 32-bit elements; how exact they have to be, the bound alone decides.
No kernel may reach another device: no remote copies, remote signals or barrier semaphores. Data moves between devices by JAX's collectives and lax.ppermute only.
A program may use at most 64 MiB of HBM per device.

```python
import jax
import jax.numpy as jnp
from jax import lax

W = 512
NRHS = 128
LEVELS = 4
KB = 1
K = 32
KC = 2
N_PROW = 32
N_PCOL = 16


def triangle_draw(key, lower_side, unit):
    first_key, second_key = jax.random.split(key)
    random_part = jax.random.normal(first_key, (K, W, W), jnp.float32)
    diagonal_part = jax.random.uniform(second_key, (K, W, 1), jnp.float32, 0.6, 1.4)
    rows_at = jnp.arange(W)[:, None]
    cols_at = jnp.arange(W)[None, :]
    if lower_side:
        keep = (rows_at > cols_at).astype(jnp.float32)
    else:
        keep = (rows_at < cols_at).astype(jnp.float32)
    identity = (rows_at == cols_at).astype(jnp.float32)
    if unit:
        main = identity[None, :, :]
    else:
        main = identity[None, :, :] * diagonal_part
    whole = main + 0.6 * keep[None, :, :] * random_part / jnp.sqrt(W * 1.0)
    return whole.reshape(K // KB, KB, W, W).astype(jnp.bfloat16)


def draw_upper_inverse(key, part):
    key = jax.random.fold_in(key, 2)
    return triangle_draw(key, True, False)


def draw_lower_inverse(key, part):
    key = jax.random.fold_in(key, 3)
    return triangle_draw(key, False, True)


def draw_parents(key, part):
    key = jax.random.fold_in(key, 5)
    positions = jnp.arange(K, dtype=jnp.int32)
    level_of = jnp.zeros((K,), jnp.int32)
    for depth_step in range(1, LEVELS):
        level_of = level_of + (positions >= K - K // 2 ** depth_step).astype(jnp.int32)
    next_start = K - jnp.right_shift(jnp.int32(K), level_of + 1)
    next_count = jnp.where(level_of + 1 < LEVELS - 1, jnp.right_shift(jnp.int32(K), level_of + 2), K // 2 ** (LEVELS - 1))
    random_pick = jax.random.randint(key, (K,), 0, 1 << 20, dtype=jnp.int32)
    random_pick = jnp.where(positions == 0, 0, random_pick)
    chosen = next_start + random_pick % jnp.maximum(next_count, 1)
    return jnp.where(level_of == LEVELS - 1, K, chosen).astype(jnp.int32)


def touch_ends(drawn, rng, low, largest):
    index_at = [jax.random.randint(jax.random.fold_in(rng, axis), (), 0, length) for axis, length in enumerate(drawn.shape)]
    widest = drawn.shape.index(max(drawn.shape))
    beside = index_at[:widest] + [(index_at[widest] + 1) % drawn.shape[widest]] + index_at[widest + 1:]
    return drawn.at[tuple(index_at)].set(low).at[tuple(beside)].set(largest)


def block_levels(own_key, shape, cuts, least, top_value):
    def one(dim, parts):
        draws = jax.random.uniform(jax.random.fold_in(jax.random.fold_in(own_key, 6), dim), (parts,), jnp.float32, least / len(cuts), top_value / len(cuts))
        return jnp.repeat(jnp.exp(draws), shape[dim] // parts).reshape((-1,) + (1,) * (len(shape) - dim - 1))

    level = one(*cuts[0])
    for cut in cuts[1:]:
        level = level * one(*cut)
    return level


def centred(stream_key, dims, scale, reach, cuts=(), kind=jnp.bfloat16):
    array = jax.random.normal(stream_key, dims, jnp.float32) * scale
    if len(cuts) > 0:
        array = block_levels(stream_key, dims, cuts, -0.22, 0.18) * array
    return jnp.clip(array, min=-reach, max=reach).astype(kind)


def setup_inputs(seed: int = 0) -> dict:
    key_list = jax.random.split(jax.random.key(seed), 7)
    factor = centred(key_list[0], (N_PROW, KB, N_PCOL, KC, W, W), (4 * W) ** -0.5, 0.125, ((0, 32), (2, 16)))
    rhs = centred(key_list[1], (N_PROW, KB, W, NRHS), 1.0, 6.0, ((0, 32),), jnp.float32)
    upper_inverse = draw_upper_inverse(jax.random.fold_in(key_list[6], 71), 0)
    lower_inverse = draw_lower_inverse(jax.random.fold_in(key_list[6], 71), 0)
    parents = draw_parents(jax.random.fold_in(key_list[6], 71), 0)
    block_mask = touch_ends((jax.random.randint(key_list[5], (K, K), 0, 4) < 3).astype(jnp.int32), jax.random.fold_in(key_list[5], 1), 0, 1)
    return dict(factor=factor, rhs=rhs, upper_inverse=upper_inverse, lower_inverse=lower_inverse, parents=parents, block_mask=block_mask)


def level_ranges(count_blocks):
    spans = []
    for depth_step in range(LEVELS - 1):
        spans.append((count_blocks - count_blocks // 2 ** depth_step, count_blocks - count_blocks // 2 ** (depth_step + 1)))
    spans.append((count_blocks - count_blocks // 2 ** (LEVELS - 1), count_blocks))
    return spans


def patterns(parents, block_mask):
    count_blocks = parents.shape[0]
    positions = jnp.arange(count_blocks, dtype=jnp.int32)
    step_matrix = (parents[:, None] == positions[None, :]).astype(jnp.float32)
    identity = jnp.eye(count_blocks, dtype=jnp.float32)
    power_now = identity
    ancestry = identity
    for depth_step in range(LEVELS - 1):
        power_now = jnp.dot(power_now, step_matrix, precision=lax.Precision.HIGHEST)
        ancestry = ancestry + power_now
    ancestry = jnp.minimum(ancestry, 1.0)
    weights = block_mask.astype(jnp.float32) * (1.0 - identity)
    return weights * ancestry, weights * ancestry.T


def reference(factor, rhs, upper_inverse, lower_inverse, parents, block_mask):
    count_blocks = K
    upper_use, lower_use = patterns(parents, block_mask)
    source_rhs = jnp.transpose(rhs, (1, 0, 2, 3)).reshape(count_blocks, W, NRHS)
    up_inv = jnp.transpose(upper_inverse, (1, 0, 2, 3)).reshape(count_blocks, W, W).astype(jnp.float32)
    low_inv = jnp.transpose(lower_inverse, (1, 0, 2, 3)).reshape(count_blocks, W, W).astype(jnp.float32)

    def column_blocks(column):
        picked = factor[:, :, column % N_PCOL, column // N_PCOL]
        return jnp.transpose(picked, (1, 0, 2, 3)).reshape(count_blocks, W, W).astype(jnp.float32)

    def sweep(base, inverse, use, order):
        solved = jnp.zeros((count_blocks, W, NRHS), jnp.float32)
        for lower_end, upper_end in order:
            for column in range(lower_end, upper_end):
                scaled = solved * use[:, column][:, None, None]
                update = jnp.einsum("iab,ian->bn", column_blocks(column), scaled, precision=lax.Precision.HIGHEST)
                value = jnp.dot(inverse[column], base[column] - update, precision=lax.Precision.HIGHEST)
                solved = solved.at[column].set(value)
        return solved

    spans = level_ranges(count_blocks)
    forward = sweep(source_rhs, up_inv, upper_use, spans)
    backward = sweep(forward, low_inv, lower_use, spans[::-1])
    return jnp.transpose(backward.reshape(KB, N_PROW, W, NRHS), (1, 0, 2, 3))
```

```python
import jax
import jax.numpy as jnp
from jax import lax
from jax.sharding import Mesh, PartitionSpec as P

LEVELS = 4
HALF = ("xl", "z")
ROW = ("xh", "xl", "z")
COL = ("y", "core")


def patterns(parents, block_mask):
    count = parents.shape[0]
    positions = jnp.arange(count, dtype=jnp.int32)
    step = (parents[:, None] == positions[None, :]).astype(jnp.float32)
    identity = jnp.eye(count, dtype=jnp.float32)
    power = identity
    ancestry = identity
    for _ in range(LEVELS - 1):
        power = jnp.dot(power, step, precision=lax.Precision.HIGHEST)
        ancestry = ancestry + power
    ancestry = jnp.minimum(ancestry, 1.0)
    weights = block_mask.astype(jnp.float32) * (1.0 - identity)
    return weights * ancestry, weights * ancestry.T


def mm(matrix, panel):
    return jnp.dot(
        matrix.astype(jnp.float32), panel, precision=lax.Precision.HIGHEST
    )


def weighted(weights, received):
    return jnp.sum(weights[:, None, None] * received, axis=0)


def a2a(array, axes):
    return lax.all_to_all(array, axes, 0, 0, tiled=True)


def spread(piece, ny):
    rows, cols = piece.shape
    copies = jnp.broadcast_to(piece[None], (ny, rows, cols))
    half = a2a(copies, "y").reshape(ny * rows, cols)
    return lax.all_gather(half, "core", tiled=True)


def per_device(factor, rhs, upper_inverse, lower_inverse, parents, block_mask):
    ny, nc, nz = lax.axis_size("y"), lax.axis_size("core"), lax.axis_size("z")
    ncol = ny * nc
    slot0 = factor[0, 0, 0, 0]
    slot1 = factor[0, 0, 0, 1]
    base = rhs[0, 0]
    up = upper_inverse[0, 0]
    low = lower_inverse[0, 0]
    width, nrhs = base.shape
    piece = width // ncol
    count = parents.shape[0]
    top = count // 2
    row = lax.axis_index(ROW)
    col = lax.axis_index(COL)
    high = (lax.axis_index("xh") == 1).astype(jnp.float32)
    last = high * (lax.axis_index("xl") == 1).astype(jnp.float32)
    upper_use, lower_use = patterns(parents, block_mask)
    to_me_u = lax.dynamic_index_in_dim(upper_use, row, 1, keepdims=False)
    to_me_l = lax.dynamic_index_in_dim(lower_use, row, 1, keepdims=False)
    to_col_l = lax.dynamic_index_in_dim(lower_use, col, 1, keepdims=False)
    mine_u = lax.dynamic_index_in_dim(upper_use, row, 0, keepdims=False)
    mine_l = lax.dynamic_index_in_dim(lower_use, row, 0, keepdims=False)
    mine = (mine_u + mine_l)[top:]

    sent = slot1.T.astype(jnp.float32).reshape(nc, ny, piece, width)
    sent = jnp.transpose(sent, (1, 0, 2, 3)).reshape(ncol, piece, width)
    slices = a2a(sent, COL)
    slices = (slices * mine[:, None, None]).astype(jnp.bfloat16).reshape(width, width)

    def updates(panel):
        return mm(slices, panel).reshape(top, piece, nrhs)

    y = mm(up, base)
    out = updates(y)
    got = a2a(jnp.concatenate([jnp.zeros_like(out), out], 0), ROW)
    w = jnp.where(jnp.arange(count) < top, to_me_u, 0.0)
    part = weighted(w, got)
    y = mm(up, base - spread(part, ny))
    got = a2a(updates(y), HALF)
    w = jnp.where(jnp.arange(top) < top // 2, to_me_u[top:], 0.0) * high
    part = part + weighted(w, got)
    y = mm(up, base - spread(part, ny))
    got = a2a(updates(y)[top // 2:], "z")
    w = jnp.where(jnp.arange(nz) < nz // 2, to_me_u[top + top // 2:], 0.0) * last
    part = part + weighted(w, got)
    y = mm(up, base - spread(part, ny))
    x = mm(low, y)
    got = a2a(updates(x)[top // 2:], "z")
    w = to_me_l[top + top // 2:] * last
    x = mm(low, y - spread(weighted(w, got), ny))
    got = a2a(updates(x), HALF)
    w = to_me_l[top:] * high
    known = spread(weighted(w, got), ny)
    x = mm(low, y - known)
    full = lax.dot_general(
        slot0.astype(jnp.float32), x, (((0,), (0,)), ((), ())), precision=lax.Precision.HIGHEST
    )
    small = width // count
    got = a2a(full.reshape(count, small, nrhs), ROW)
    part = weighted(to_col_l, got)
    copies = lax.all_gather(part[None], "core", tiled=True)
    copies = jnp.broadcast_to(copies[None], (ny,) + copies.shape)
    every = a2a(copies, "y").reshape(ncol, small, nrhs)
    got = a2a(jnp.concatenate([every, jnp.zeros_like(every)], 0), ROW).reshape(width, nrhs)
    x = mm(low, y - known - got)
    return x[None, None]


def solution(mesh):
    grid = Mesh(mesh.devices.reshape(2, 2, 8, 8, 2), ("xh", "xl", "z", "y", "core"))
    placed = (
        P(ROW, None, COL, None, None, None),
        P(ROW, None, None, None),
        P(ROW, None, None, None),
        P(ROW, None, None, None),
        P(),
        P(),
    )
    return jax.shard_map(
        per_device,
        mesh=grid,
        in_specs=placed,
        out_specs=P(ROW, None, None, None),
        check_vma=False,
    )
```

```python
import jax
import jax.numpy as jnp
from jax import lax
from jax.sharding import Mesh, PartitionSpec as P

LEVELS = 4
HALF = ("xl", "z")
ROW = ("xh", "xl", "z")
COL = ("y", "core")


def patterns(parents, block_mask):
    count = parents.shape[0]
    positions = jnp.arange(count, dtype=jnp.int32)
    step = (parents[:, None] == positions[None, :]).astype(jnp.float32)
    identity = jnp.eye(count, dtype=jnp.float32)
    power = identity
    ancestry = identity
    for _ in range(LEVELS - 1):
        power = jnp.dot(power, step, precision=lax.Precision.HIGHEST)
        ancestry = ancestry + power
    ancestry = jnp.minimum(ancestry, 1.0)
    weights = block_mask.astype(jnp.float32) * (1.0 - identity)
    return weights * ancestry, weights * ancestry.T


def mm(matrix, panel):
    return jnp.dot(
        matrix.astype(jnp.float32), panel, precision=lax.Precision.HIGHEST
    )


def weighted(weights, received):
    return jnp.sum(weights[:, None, None] * received, axis=0)


def a2a(array, axes):
    return lax.all_to_all(array, axes, 0, 0, tiled=True)


def spread(piece, ny):
    rows, cols = piece.shape
    copies = jnp.broadcast_to(piece[None], (ny, rows, cols))
    half = a2a(copies, "y").reshape(ny * rows, cols)
    return lax.all_gather(half, "core", tiled=True)


def per_device(factor, rhs, upper_inverse, lower_inverse, parents, block_mask):
    ny, nc, nz = lax.axis_size("y"), lax.axis_size("core"), lax.axis_size("z")
    ncol = ny * nc
    slot0 = factor[0, 0, 0, 0]
    slot1 = factor[0, 0, 0, 1]
    base = rhs[0, 0]
    up = upper_inverse[0, 0]
    low = lower_inverse[0, 0]
    width, nrhs = base.shape
    piece = width // ncol
    count = parents.shape[0]
    top = count // 2
    row = lax.axis_index(ROW)
    col = lax.axis_index(COL)
    high = (lax.axis_index("xh") == 1).astype(jnp.float32)
    last = high * (lax.axis_index("xl") == 1).astype(jnp.float32)
    upper_use, lower_use = patterns(parents, block_mask)
    to_me_u = lax.dynamic_index_in_dim(upper_use, row, 1, keepdims=False)
    to_me_l = lax.dynamic_index_in_dim(lower_use, row, 1, keepdims=False)
    to_col_u = lax.dynamic_index_in_dim(upper_use, top + col, 1, keepdims=False)
    mine_u = lax.dynamic_index_in_dim(upper_use, row, 0, keepdims=False)
    mine_l = lax.dynamic_index_in_dim(lower_use, row, 0, keepdims=False)
    mine = (mine_u + mine_l)[top:]

    def resliced(block, use):
        sent = block.T.astype(jnp.float32).reshape(nc, ny, piece, width)
        sent = jnp.transpose(sent, (1, 0, 2, 3)).reshape(ncol, piece, width)
        got = a2a(sent, COL) * use[:, None, None]
        return got.astype(jnp.bfloat16).reshape(width, width)

    slices = resliced(slot1, (mine_u + mine_l)[top:])
    slices0 = resliced(slot0, mine_l[:top])

    def updates(panel):
        return mm(slices, panel).reshape(top, piece, nrhs)

    y = mm(up, base)
    full = lax.dot_general(
        slot1.astype(jnp.float32), y, (((0,), (0,)), ((), ())), precision=lax.Precision.HIGHEST
    )
    small = width // count
    got = a2a(full.reshape(count, small, nrhs), ROW)
    w = jnp.where(jnp.arange(count) < top, to_col_u, 0.0)
    part = weighted(w, got)
    copies = lax.all_gather(part[None], "core", tiled=True)
    copies = jnp.broadcast_to(copies[None], (ny,) + copies.shape)
    every = a2a(copies, "y").reshape(ncol, small, nrhs)
    known = a2a(jnp.concatenate([jnp.zeros_like(every), every], 0), ROW).reshape(width, nrhs)
    y = mm(up, base - known)
    got = a2a(updates(y), HALF)
    w = jnp.where(jnp.arange(top) < top // 2, to_me_u[top:], 0.0) * high
    part = weighted(w, got)
    y = mm(up, base - known - spread(part, ny))
    got = a2a(updates(y)[top // 2:], "z")
    w = jnp.where(jnp.arange(nz) < nz // 2, to_me_u[top + top // 2:], 0.0) * last
    part = part + weighted(w, got)
    y = mm(up, base - known - spread(part, ny))
    x = mm(low, y)
    got = a2a(updates(x)[top // 2:], "z")
    w = to_me_l[top + top // 2:] * last
    x = mm(low, y - spread(weighted(w, got), ny))
    got = a2a(updates(x), HALF)
    w = to_me_l[top:] * high
    known = spread(weighted(w, got), ny)
    x = mm(low, y - known)
    out = mm(slices0, x).reshape(top, piece, nrhs)
    got = a2a(jnp.concatenate([out, jnp.zeros_like(out)], 0), ROW)
    rest = spread(weighted(to_me_l, got) * (1.0 - high), ny)
    x = mm(low, y - known - rest)
    return x[None, None]


def solution(mesh):
    grid = Mesh(mesh.devices.reshape(2, 2, 8, 8, 2), ("xh", "xl", "z", "y", "core"))
    placed = (
        P(ROW, None, COL, None, None, None),
        P(ROW, None, None, None),
        P(ROW, None, None, None),
        P(ROW, None, None, None),
        P(),
        P(),
    )
    return jax.shard_map(
        per_device,
        mesh=grid,
        in_specs=placed,
        out_specs=P(ROW, None, None, None),
        check_vma=False,
    )
```

```python
import jax
import jax.numpy as jnp
from jax import lax
from jax.sharding import Mesh, PartitionSpec as P

LEVELS = 4
HALF = ("xl", "z")
ROW = ("xh", "xl", "z")
COL = ("y", "core")


def patterns(parents, block_mask):
    count = parents.shape[0]
    positions = jnp.arange(count, dtype=jnp.int32)
    step = (parents[:, None] == positions[None, :]).astype(jnp.float32)
    identity = jnp.eye(count, dtype=jnp.float32)
    power = identity
    ancestry = identity
    for _ in range(LEVELS - 1):
        power = jnp.dot(power, step, precision=lax.Precision.HIGHEST)
        ancestry = ancestry + power
    ancestry = jnp.minimum(ancestry, 1.0)
    weights = block_mask.astype(jnp.float32) * (1.0 - identity)
    return weights * ancestry, weights * ancestry.T


def mm(matrix, panel):
    return jnp.dot(
        matrix.astype(jnp.float32), panel, precision=lax.Precision.HIGHEST
    )


def weighted(weights, received):
    return jnp.sum(weights[:, None, None] * received, axis=0)


def a2a(array, axes):
    array = lax.optimization_barrier(array)
    return lax.optimization_barrier(lax.all_to_all(array, axes, 0, 0, tiled=True))


def spread(piece, ny):
    rows, cols = piece.shape
    copies = jnp.broadcast_to(piece[None], (ny, rows, cols))
    half = a2a(copies, "y").reshape(ny * rows, cols)
    return lax.all_gather(half, "core", tiled=True)


def per_device(factor, rhs, upper_inverse, lower_inverse, parents, block_mask):
    ny, nc, nz = lax.axis_size("y"), lax.axis_size("core"), lax.axis_size("z")
    ncol = ny * nc
    slot0 = factor[0, 0, 0, 0]
    slot1 = factor[0, 0, 0, 1]
    base = rhs[0, 0]
    up = upper_inverse[0, 0]
    low = lower_inverse[0, 0]
    width, nrhs = base.shape
    piece = width // ncol
    count = parents.shape[0]
    top = count // 2
    row = lax.axis_index(ROW)
    col = lax.axis_index(COL)
    high = (lax.axis_index("xh") == 1).astype(jnp.float32)
    last = high * (lax.axis_index("xl") == 1).astype(jnp.float32)
    upper_use, lower_use = patterns(parents, block_mask)
    to_me_u = lax.dynamic_index_in_dim(upper_use, row, 1, keepdims=False)
    to_me_l = lax.dynamic_index_in_dim(lower_use, row, 1, keepdims=False)
    to_col_l = lax.dynamic_index_in_dim(lower_use, col, 1, keepdims=False)
    mine_u = lax.dynamic_index_in_dim(upper_use, row, 0, keepdims=False)
    mine_l = lax.dynamic_index_in_dim(lower_use, row, 0, keepdims=False)
    mine = (mine_u + mine_l)[top:]

    ranks = jnp.arange(count)
    w_all = jnp.where(ranks < top, to_me_u, 0.0)
    w_one = jnp.where(ranks[:top] < top // 2, to_me_u[top:], 0.0) * high
    w_two = jnp.where(ranks[:nz] < nz // 2, to_me_u[top + top // 2:], 0.0) * last
    w_three = to_me_l[top + top // 2:] * last
    w_down = to_me_l[top:] * high
    y = mm(up, base)

    sent = slot1.T.astype(jnp.float32).reshape(nc, ny, piece, width)
    sent = jnp.transpose(sent, (1, 0, 2, 3)).reshape(ncol, piece, width)
    first = (sent, y, mine, w_all, w_one, w_two, w_three, w_down, to_col_l, base, up, low)
    sent, y, mine, w_all, w_one, w_two, w_three, w_down, to_col_l, base, up, low = (
        lax.optimization_barrier(first)
    )
    slices = a2a(sent, COL)
    slices = (slices * mine[:, None, None]).astype(jnp.bfloat16).reshape(width, width)

    def updates(panel):
        return mm(slices, panel).reshape(top, piece, nrhs)

    out = updates(y)
    got = a2a(jnp.concatenate([jnp.zeros_like(out), out], 0), ROW)
    part = weighted(w_all, got)
    y = mm(up, base - spread(part, ny))
    got = a2a(updates(y), HALF)
    part = part + weighted(w_one, got)
    y = mm(up, base - spread(part, ny))
    got = a2a(updates(y)[top // 2:], "z")
    part = part + weighted(w_two, got)
    y = mm(up, base - spread(part, ny))
    x = mm(low, y)
    got = a2a(updates(x)[top // 2:], "z")
    x = mm(low, y - spread(weighted(w_three, got), ny))
    got = a2a(updates(x), HALF)
    known = spread(weighted(w_down, got), ny)
    x = mm(low, y - known)
    full = lax.dot_general(
        slot0.astype(jnp.float32), x, (((0,), (0,)), ((), ())), precision=lax.Precision.HIGHEST
    )
    small = width // count
    got = a2a(full.reshape(count, small, nrhs), ROW)
    part = weighted(to_col_l, got)
    copies = lax.all_gather(part[None], "core", tiled=True)
    copies = jnp.broadcast_to(copies[None], (ny,) + copies.shape)
    every = a2a(copies, "y").reshape(ncol, small, nrhs)
    got = a2a(jnp.concatenate([every, jnp.zeros_like(every)], 0), ROW).reshape(width, nrhs)
    x = mm(low, y - known - got)
    return x[None, None]


def solution(mesh):
    grid = Mesh(mesh.devices.reshape(2, 2, 8, 8, 2), ("xh", "xl", "z", "y", "core"))
    placed = (
        P(ROW, None, COL, None, None, None),
        P(ROW, None, None, None),
        P(ROW, None, None, None),
        P(ROW, None, None, None),
        P(),
        P(),
    )
    return jax.shard_map(
        per_device,
        mesh=grid,
        in_specs=placed,
        out_specs=P(ROW, None, None, None),
        check_vma=False,
    )
```

```python
import jax
import jax.numpy as jnp
import numpy as np
from jax import lax
from jax.sharding import Mesh, PartitionSpec as P

LEVELS = 4
HALF = ("xl", "z")
ROW = ("xh", "xl", "z")
COL = ("y", "core")
HIGHEST = lax.Precision.HIGHEST


def patterns(parents, block_mask):
    count = parents.shape[0]
    positions = jnp.arange(count, dtype=jnp.int32)
    step = (parents[:, None] == positions[None, :]).astype(jnp.float32)
    identity = jnp.eye(count, dtype=jnp.float32)
    power = identity
    ancestry = identity
    for _ in range(LEVELS - 1):
        power = jnp.dot(power, step, precision=HIGHEST)
        ancestry = ancestry + power
    ancestry = jnp.minimum(ancestry, 1.0)
    weights = block_mask.astype(jnp.float32) * (1.0 - identity)
    return weights * ancestry, weights * ancestry.T, ancestry


def mm(matrix, panel):
    return jnp.dot(matrix.astype(jnp.float32), panel, precision=HIGHEST)


def mt(panel, matrix):
    return lax.dot_general(
        panel, matrix.astype(jnp.float32), (((1,), (1,)), ((), ())), precision=HIGHEST
    )


def weighted(weights, received):
    return jnp.sum(weights[:, None, None] * received, axis=0)


def a2a(array, axes):
    array = lax.optimization_barrier(array)
    return lax.optimization_barrier(lax.all_to_all(array, axes, 0, 0, tiled=True))


def copies(array, times):
    return jnp.broadcast_to(array[None], (times,) + array.shape)


def over_columns(array, ny):
    both = lax.all_gather(array[None], "core", tiled=True)
    return a2a(copies(both, ny), "y")


def per_device(factor, rhs, upper_inverse, lower_inverse, parents, block_mask):
    ny, nc, nz = lax.axis_size("y"), lax.axis_size("core"), lax.axis_size("z")
    ncol = ny * nc
    slot0 = factor[0, 0, 0, 0]
    slot1 = factor[0, 0, 0, 1]
    base = rhs[0, 0]
    up = upper_inverse[0, 0]
    low = lower_inverse[0, 0]
    width, nrhs = base.shape
    piece = width // ncol
    mine_rhs = nrhs // ncol
    count = parents.shape[0]
    top = count // 2
    small = width // count
    row = lax.axis_index(ROW)
    col = lax.axis_index(COL)
    zat = lax.axis_index("z")
    is_high = lax.axis_index("xh") == 1
    high = is_high.astype(jnp.float32)
    last = high * (lax.axis_index("xl") == 1).astype(jnp.float32)
    levels_np = np.zeros(count, np.int32)
    for level in range(1, LEVELS):
        levels_np[count - count // 2**level:] = level
    level_of = jnp.asarray(levels_np)
    my_level = level_of[row]
    is_one = high * (my_level == 1)
    upper_use, lower_use, ancestry = patterns(parents, block_mask)

    def column(table, at):
        return lax.dynamic_index_in_dim(table, at, 1, keepdims=False)

    def line(table, at):
        return lax.dynamic_index_in_dim(table, at, 0, keepdims=False)

    w_all = jnp.where(level_of == 0, column(upper_use, row), 0.0)
    to_col_l = column(lower_use, col)
    above_u = line(upper_use, row)[top:]
    used = (line(upper_use, row) + line(lower_use, row))[top:]
    above_l = column(lower_use, row)[top:]
    above = line(ancestry, row)[top:] * high
    lev_top = level_of[top:]
    pick_u = [jnp.where(lev_top == level, above_u, 0.0) for level in (2, 3)]
    pick_l = [jnp.where(lev_top == level, above_l, 0.0) for level in (2, 3)]
    send_to = [jnp.where(lev_top == level, above, 0.0) * is_one for level in (2, 3)]
    take = [jnp.where(lev_top == level, above, 0.0) for level in (2, 3)]
    roots = jnp.where(level_of == 3, jnp.arange(count, dtype=jnp.int32), parents)[count - nz:]
    family = (roots == roots[zat]).astype(jnp.float32) * last

    y0 = mm(up, base)
    base_t = lax.dynamic_slice_in_dim(base.T, col * mine_rhs, mine_rhs, 0)
    both = jnp.dot(low, up, preferred_element_type=jnp.float32)
    sent = slot1.T.astype(jnp.float32).reshape(ncol, piece, width)
    (sent, y0, base_t, both, up, low, used, w_all, to_col_l, pick_u, pick_l, send_to, take, family) = (
        lax.optimization_barrier(
            (sent, y0, base_t, both, up, low, used, w_all, to_col_l, pick_u, pick_l, send_to, take, family)
        )
    )

    slices = a2a(sent, COL)

    def gathered(weights, pieces):
        local = jnp.concatenate([weighted(w, pieces) for w in weights], 0)
        return lax.all_gather(local, COL, tiled=True)

    def apart(product):
        split = product.reshape(mine_rhs, ncol, 2, piece)
        return jnp.transpose(split, (2, 0, 1, 3)).reshape(2, mine_rhs, width)

    blocks_u = gathered(pick_u, slices)
    half = top // 2
    quarter = top // 4
    roots_part = slices[half:half + quarter].reshape(quarter * piece, width)
    roots_part = mm(roots_part, both).reshape(quarter, piece, width)
    middle = jnp.where(my_level == 3, roots_part, slices[half:half + quarter])
    down = jnp.concatenate([slices[:half], middle, slices[half + quarter:]], 0)
    blocks_l = gathered(pick_l, a2a(down, HALF))

    own = (slices * used[:, None, None]).astype(jnp.bfloat16).reshape(width, width)
    out = mm(own, y0).reshape(top, piece, nrhs)
    got = a2a(jnp.concatenate([jnp.zeros_like(out), out], 0), ROW)
    part = weighted(w_all, got).T.reshape(ncol, mine_rhs, piece)
    part = jnp.transpose(a2a(part, COL), (1, 0, 2)).reshape(mine_rhs, width)
    rest = base_t - part * high
    y = mt(rest, up)
    parts = apart(mt(y, blocks_u))
    out = send_to[0][:, None, None] * parts[0] + send_to[1][:, None, None] * parts[1]
    rest = rest - jnp.sum(a2a(out, HALF), 0) * high
    y = mt(rest, up)
    out = jnp.where(my_level == 3, rest, -apart(mt(y, blocks_u))[1])
    root = weighted(family, a2a(copies(out, nz), "z"))
    y_root = mt(root, up)
    down_root = apart(mt(root, blocks_l))[1]
    x = mt(jnp.where(my_level == 3, y_root, y - down_root), low)
    got = a2a(copies(x, top), HALF)
    two = jnp.concatenate([weighted(take[0], got), weighted(take[1], got)], 0)
    prod = lax.dot_general(
        two, blocks_l, (((1,), (1,)), ((), ())), precision=HIGHEST
    ).reshape(2, mine_rhs, ncol, 2, piece)
    update = (prod[0, :, :, 0] + prod[1, :, :, 1]).reshape(mine_rhs, width)
    x = jnp.where(my_level == 1, mt(y - update, low), x)
    x = over_columns(x, ny).reshape(nrhs, width)
    full = lax.dot_general(
        slot0.astype(jnp.float32), x, (((0,), (1,)), ((), ())), precision=HIGHEST
    )
    got = a2a(full.reshape(count, small, nrhs), ROW)
    every = over_columns(weighted(to_col_l, got), ny).reshape(ncol, small, nrhs)
    got = a2a(jnp.concatenate([every, jnp.zeros_like(every)], 0), ROW).reshape(width, nrhs)
    result = jnp.where(is_high, x.T, mm(low, y0 - got))
    return result[None, None]


def solution(mesh):
    grid = Mesh(mesh.devices.reshape(2, 2, 8, 8, 2), ("xh", "xl", "z", "y", "core"))
    placed = (
        P(ROW, None, COL, None, None, None),
        P(ROW, None, None, None),
        P(ROW, None, None, None),
        P(ROW, None, None, None),
        P(),
        P(),
    )
    return jax.shard_map(
        per_device,
        mesh=grid,
        in_specs=placed,
        out_specs=P(ROW, None, None, None),
        check_vma=False,
    )
```

```python
import functools

import jax
import jax.numpy as jnp
from jax import lax
from jax.experimental import pallas as pl
from jax.experimental.pallas import tpu as pltpu
from jax.sharding import Mesh, PartitionSpec as P

LEVELS = 4
HALF = ("xl", "z")
ROW = ("xh", "xl", "z")
COL = ("y", "core")
HIGHEST = lax.Precision.HIGHEST
F32 = jnp.float32
BF16 = jnp.bfloat16
ROOMY = pltpu.CompilerParams(vmem_limit_bytes=40 * 1024 * 1024)

FROM_LEAF, FROM_LOW, PICK_TWO, PICK_THREE, BELOW, SEND_TWO, SEND_THREE, SEND_ROOT, FLAGS = range(9)


def call(body, shape, specs, *args, scratch=()):
    many = isinstance(shape, tuple)
    out = [pl.BlockSpec(memory_space=pltpu.VMEM)] * len(shape) if many else pl.BlockSpec(
        memory_space=pltpu.VMEM
    )
    return pl.pallas_call(
        body,
        out_shape=shape,
        in_specs=specs,
        out_specs=out,
        scratch_shapes=list(scratch),
        compiler_params=ROOMY,
    )(*args)


VM = pl.BlockSpec(memory_space=pltpu.VMEM)
SM = pl.BlockSpec(memory_space=pltpu.SMEM)
HB = pl.BlockSpec(memory_space=pl.ANY)


def fetch(blocks, held, arrived, start):
    copy = pltpu.make_async_copy(blocks.at[:, pl.ds(start, held.shape[1])], held, arrived)
    copy.start()
    return copy


def room(blocks, slots):
    shape = (blocks.shape[0], slots) + blocks.shape[2:]
    return [pltpu.VMEM(shape, F32), pltpu.SemaphoreType.DMA]


def shape_of(*dims, kind=F32):
    return jax.ShapeDtypeStruct(dims, kind)


def three(panel):
    high = panel.astype(BF16).astype(F32)
    rest = panel - high
    mid = rest.astype(BF16).astype(F32)
    return high, mid, rest - mid


def mt(panel, matrix):
    rows = panel.shape[0]
    parts = jnp.concatenate(three(panel), 0).astype(BF16)
    product = lax.dot_general(
        parts, matrix, (((1,), (1,)), ((), ())), preferred_element_type=F32
    )
    return product[:rows] + product[rows:2 * rows] + product[2 * rows:]


def table_kernel(at, parents_row, parents_col, mask, mask_t, out):
    count = mask.shape[0]
    top = count // 2
    row, col = at[0], at[1]
    down = lax.broadcasted_iota(jnp.int32, (count, count), 0)
    across = lax.broadcasted_iota(jnp.int32, (count, count), 1)
    step = (parents_col[...] == across).astype(F32)
    step_t = (parents_row[...] == down).astype(F32)
    identity = (down == across).astype(F32)
    anc = power = anc_t = power_t = identity
    for _ in range(LEVELS - 1):
        power = jnp.dot(power, step, preferred_element_type=F32)
        power_t = jnp.dot(step_t, power_t, preferred_element_type=F32)
        anc = anc + power
        anc_t = anc_t + power_t
    anc = jnp.minimum(anc, 1.0)
    anc_t = jnp.minimum(anc_t, 1.0)
    weights = mask[...].astype(F32) * (1.0 - identity)
    weights_t = mask_t[...].astype(F32) * (1.0 - identity)

    def line(matrix, index):
        return jnp.sum(jnp.where(down == index, matrix, 0.0), axis=0, keepdims=True)

    def level(ids):
        total = jnp.zeros_like(ids)
        for depth in range(1, LEVELS):
            total = total + (ids >= count - count // 2**depth).astype(jnp.int32)
        return total

    levels = level(lax.broadcasted_iota(jnp.int32, (1, count), 1))
    mine = level(jnp.full((1, count), row, jnp.int32))
    two = (levels == 2).astype(F32)
    three_ = (levels == 3).astype(F32)
    one_mine = (mine == 1).astype(F32)
    two_mine = (mine == 2).astype(F32)
    late = (mine >= 2).astype(F32)
    use_row = line(weights * anc, row)
    above = line(anc, row)
    rows = [
        line(weights_t * anc_t, row) * (levels == 0).astype(F32),
        line(weights_t * anc, col),
        use_row * two * one_mine,
        use_row * three_ * (one_mine + two_mine),
        line(weights * anc_t, row) * late,
        above * two * one_mine,
        above * three_ * one_mine,
        above * three_ * two_mine,
        jnp.where(
            lax.broadcasted_iota(jnp.int32, (1, count), 1) == 0,
            (mine >= 1).astype(F32),
            (mine == 3).astype(F32),
        ),
    ]
    rows = rows + [jnp.zeros((1, count), F32)] * (out.shape[0] - len(rows))
    out[...] = jnp.concatenate(rows, 0)


def first_kernel(table, slices, y0, out, local_a, local_b):
    top, piece, width = slices.shape
    nrhs = y0.shape[1]
    half, quarter = top // 2, top // 4
    is_root = table[FLAGS, 1]
    own = slices[...].reshape(top * piece, width).astype(BF16)
    parts = jnp.concatenate(three(y0[...]), 1).astype(BF16)
    product = jnp.dot(own, parts, preferred_element_type=F32)
    product = product[:, :nrhs] + product[:, nrhs:2 * nrhs] + product[:, 2 * nrhs:]
    out[:top] = jnp.zeros((top, piece, nrhs), F32)
    out[top:] = product.reshape(top, piece, nrhs)
    for slot in range(quarter):
        total = (table[BELOW, top + half + slot] * is_root) * slices[half + slot]
        if slot < 2:
            line = (PICK_TWO, PICK_THREE)[slot]
            start = half + slot * quarter
            for k in range(start, start + quarter):
                total = total + table[line, top + k] * slices[k]
        local_a[0, slot] = total
    for k in range(half):
        local_b[0, k] = table[BELOW, top + k] * slices[k]


def leaf_kernel(table, got, out):
    total = table[FROM_LEAF, 0] * got[0]
    for k in range(1, got.shape[0] // 2):
        total = total + table[FROM_LEAF, k] * got[k]
    out[...] = total.T


def level_one_kernel(table, got, base_t, up, blocks, rest_out, y_out, out, held, arrived):
    copy = fetch(blocks, held, arrived, 0)
    pieces, rhs, piece = got.shape
    top = out.shape[0]
    width = base_t.shape[1]
    part = jnp.concatenate([got[k] for k in range(pieces)], 1)
    rest = base_t[...] - part * table[FLAGS, 0]
    y = mt(rest, up[...])
    rest_out[...] = rest
    y_out[...] = y
    copy.wait()
    a = mt(y, held[:, 0].reshape(width, width).astype(BF16))
    b = mt(y, held[:, 1].reshape(width, width).astype(BF16))
    for k in range(top):
        out[k] = table[SEND_TWO, top + k] * a + table[SEND_THREE, top + k] * b


def level_two_kernel(table, got, rest_in, up, blocks, rest_out, y_out, out, held, arrived):
    copy = fetch(blocks, held, arrived, 1)
    width = rest_in.shape[1]
    nz = out.shape[0]
    count = table.shape[1]
    rest = rest_in[...] - jnp.sum(got[...], 0)
    y = mt(rest, up[...])
    rest_out[...] = rest
    y_out[...] = y
    copy.wait()
    b = mt(y, held[:, 0].reshape(width, width).astype(BF16))
    for k in range(nz):
        out[k] = table[SEND_ROOT, count - nz + k] * b


def level_three_kernel(table, got, rest_in, up, low, blocks, y_out, out, held, arrived):
    copy = fetch(blocks, held, arrived, 0)
    width = rest_in.shape[1]
    nz = out.shape[0]
    slots = blocks.shape[1]
    rest = rest_in[...] - jnp.sum(got[...], 0)
    y = mt(rest, up[...])
    y_out[...] = y
    x = mt(y, low[...]) * table[FLAGS, 1]
    copy.wait()
    for k in range(slots):
        out[k] = mt(x, held[:, k].reshape(width, width).astype(BF16))
    for k in range(slots, nz):
        out[k] = jnp.zeros_like(x)


def down_kernel(slots, got, y_in, low, blocks, rest_out, out, x_now):
    step = pl.program_id(0)
    width = y_in.shape[1]

    @pl.when(step == 0)
    def _():
        rest = y_in[...] - jnp.sum(got[...], 0)
        rest_out[...] = rest
        x_now[...] = mt(rest, low[...])

    @pl.when(step < slots)
    def _():
        out[0] = mt(x_now[...], blocks[...].reshape(width, width).astype(BF16))

    @pl.when(step >= slots)
    def _():
        out[0] = jnp.zeros_like(x_now)


def last_kernel(got, rest_in, low, out):
    out[0] = mt(rest_in[...] - jnp.sum(got[...], 0), low[...])


def a2a(array, axes):
    array = lax.optimization_barrier(array)
    return lax.optimization_barrier(lax.all_to_all(array, axes, 0, 0, tiled=True))


def copies(array, times):
    return jnp.broadcast_to(array[None], (times,) + array.shape)


def over_columns(array, ny):
    both = lax.all_gather(array, "core", tiled=True)
    return a2a(copies(both, ny), "y")


def per_device(factor, rhs, upper_inverse, lower_inverse, parents, block_mask):
    ny, nc, nz = lax.axis_size("y"), lax.axis_size("core"), lax.axis_size("z")
    ncol = ny * nc
    slot0 = factor[0, 0, 0, 0]
    slot1 = factor[0, 0, 0, 1]
    base = rhs[0, 0]
    up = upper_inverse[0, 0]
    low = lower_inverse[0, 0]
    width, nrhs = base.shape
    piece = width // ncol
    mine = nrhs // ncol
    count = parents.shape[0]
    top = count // 2
    half, quarter = top // 2, top // 4
    small = width // count
    row = lax.axis_index(ROW)
    col = lax.axis_index(COL)
    is_high = lax.axis_index("xh") == 1

    sent = slot1.T.astype(F32).reshape(ncol, piece, width)
    table = call(
        table_kernel, shape_of(16, count), [SM, VM, VM, VM, VM],
        jnp.stack([row, col]).astype(jnp.int32), parents[None, :], parents[:, None],
        block_mask, block_mask.T,
    )
    y0 = jnp.dot(up.astype(F32), base, precision=HIGHEST)
    base_t = lax.dynamic_slice_in_dim(base.T, col * mine, mine, 0)

    slices = lax.all_to_all(sent, COL, 0, 0, tiled=True)
    table, y0, base_t, slices = lax.optimization_barrier((table, y0, base_t, slices))
    out, local_a, local_b = call(
        first_kernel,
        (
            shape_of(count, piece, nrhs),
            shape_of(1, quarter, piece, width),
            shape_of(1, half, piece, width),
        ),
        [SM, VM, VM], table, slices, y0,
    )
    blocks_a = lax.all_gather(local_a, COL, tiled=True)
    blocks_b = lax.all_gather(local_b, COL, tiled=True)

    part = call(leaf_kernel, shape_of(nrhs, piece), [SM, VM], table, a2a(out, ROW))
    got = a2a(part.reshape(ncol, mine, piece), COL)
    panel = shape_of(mine, width)
    rest, y, out = call(
        level_one_kernel, (panel, panel, shape_of(top, mine, width)), [SM, VM, VM, VM, HB],
        table, got, base_t, up, blocks_a, scratch=room(blocks_a, 2),
    )
    rest, y, out = call(
        level_two_kernel, (panel, panel, shape_of(nz, mine, width)), [SM, VM, VM, VM, HB],
        table, a2a(out, HALF), rest, up, blocks_a, scratch=room(blocks_a, 1),
    )
    y, out = call(
        level_three_kernel, (panel, shape_of(nz, mine, width)), [SM, VM, VM, VM, VM, HB],
        table, a2a(out, "z"), rest, up, low, blocks_a, scratch=room(blocks_a, quarter),
    )
    got = a2a(out, "z")
    whole = lambda array: pl.BlockSpec(array.shape, lambda k: (0,) * array.ndim)
    rest, out = pl.pallas_call(
        functools.partial(down_kernel, half),
        out_shape=(panel, shape_of(top, mine, width)),
        grid=(top,),
        in_specs=[
            whole(got), whole(y), whole(low),
            pl.BlockSpec((ncol, 1, piece, width), lambda k: (0, jnp.minimum(k, half - 1), 0, 0)),
        ],
        out_specs=(
            pl.BlockSpec((mine, width), lambda k: (0, 0)),
            pl.BlockSpec((1, mine, width), lambda k: (k, 0, 0)),
        ),
        scratch_shapes=[pltpu.VMEM((mine, width), F32)],
        compiler_params=ROOMY,
    )(got, y, low, blocks_b)
    x = call(last_kernel, shape_of(1, mine, width), [VM, VM, VM], a2a(out, HALF), rest, low)
    x = over_columns(x, ny).reshape(nrhs, width)
    full = lax.dot_general(
        slot0.astype(F32), x, (((0,), (1,)), ((), ())), precision=HIGHEST
    )
    got = a2a(full.reshape(count, small, nrhs), ROW)
    part = jnp.sum(table[FROM_LOW][:, None, None] * got, axis=0)
    every = over_columns(part[None], ny).reshape(ncol, small, nrhs)
    got = a2a(jnp.concatenate([every, jnp.zeros_like(every)], 0), ROW).reshape(width, nrhs)
    below = jnp.dot(low.astype(F32), y0 - got, precision=HIGHEST)
    return jnp.where(is_high, x.T, below)[None, None]


def solution(mesh):
    grid = Mesh(mesh.devices.reshape(2, 2, 8, 8, 2), ("xh", "xl", "z", "y", "core"))
    placed = (
        P(ROW, None, COL, None, None, None),
        P(ROW, None, None, None),
        P(ROW, None, None, None),
        P(ROW, None, None, None),
        P(),
        P(),
    )
    return jax.shard_map(
        per_device,
        mesh=grid,
        in_specs=placed,
        out_specs=P(ROW, None, None, None),
        check_vma=False,
    )
```

```python
import jax
import jax.numpy as jnp
from jax import lax
from jax.experimental import pallas as pl
from jax.experimental.pallas import tpu as pltpu
from jax.sharding import Mesh, PartitionSpec as P

LEVELS = 4
HALF = ("xl", "z")
ROW = ("xh", "xl", "z")
COL = ("y", "core")
HIGHEST = lax.Precision.HIGHEST
F32 = jnp.float32
BF16 = jnp.bfloat16
ROOMY = pltpu.CompilerParams(vmem_limit_bytes=40 * 1024 * 1024)

FROM_LEAF, FROM_LOW, PICK_TWO, PICK_THREE, BELOW, SEND_TWO, SEND_THREE, SEND_ROOT, FLAGS, ABOVE = range(10)


def call(body, shape, specs, *args, scratch=()):
    many = isinstance(shape, tuple)
    out = [pl.BlockSpec(memory_space=pltpu.VMEM)] * len(shape) if many else pl.BlockSpec(
        memory_space=pltpu.VMEM
    )
    return pl.pallas_call(
        body,
        out_shape=shape,
        in_specs=specs,
        out_specs=out,
        scratch_shapes=list(scratch),
        compiler_params=ROOMY,
    )(*args)


VM = pl.BlockSpec(memory_space=pltpu.VMEM)
SM = pl.BlockSpec(memory_space=pltpu.SMEM)
HB = pl.BlockSpec(memory_space=pltpu.HBM)


def fetch(blocks, held, arrived, start):
    copy = pltpu.make_async_copy(blocks.at[:, pl.ds(start, held.shape[1])], held, arrived)
    copy.start()
    return copy


def room(blocks, slots):
    shape = (blocks.shape[0], slots) + blocks.shape[2:]
    return [pltpu.VMEM(shape, F32), pltpu.SemaphoreType.DMA]


def shape_of(*dims, kind=F32):
    return jax.ShapeDtypeStruct(dims, kind)


def three(panel):
    high = panel.astype(BF16).astype(F32)
    rest = panel - high
    mid = rest.astype(BF16).astype(F32)
    return high, mid, rest - mid


def mt(panel, matrix):
    rows = panel.shape[0]
    parts = jnp.concatenate(three(panel), 0).astype(BF16)
    product = lax.dot_general(
        parts, matrix, (((1,), (1,)), ((), ())), preferred_element_type=F32
    )
    return product[:rows] + product[rows:2 * rows] + product[2 * rows:]


def table_kernel(at, parents_row, parents_col, mask, mask_t, out):
    count = mask.shape[0]
    top = count // 2
    row, col = at[0], at[1]
    down = lax.broadcasted_iota(jnp.int32, (count, count), 0)
    across = lax.broadcasted_iota(jnp.int32, (count, count), 1)
    step = (parents_col[...] == across).astype(F32)
    step_t = (parents_row[...] == down).astype(F32)
    identity = (down == across).astype(F32)
    anc = power = anc_t = power_t = identity
    for _ in range(LEVELS - 1):
        power = jnp.dot(power, step, preferred_element_type=F32)
        power_t = jnp.dot(step_t, power_t, preferred_element_type=F32)
        anc = anc + power
        anc_t = anc_t + power_t
    anc = jnp.minimum(anc, 1.0)
    anc_t = jnp.minimum(anc_t, 1.0)
    weights = mask[...].astype(F32) * (1.0 - identity)
    weights_t = mask_t[...].astype(F32) * (1.0 - identity)

    def line(matrix, index):
        return jnp.sum(jnp.where(down == index, matrix, 0.0), axis=0, keepdims=True)

    def level(ids):
        total = jnp.zeros_like(ids)
        for depth in range(1, LEVELS):
            total = total + (ids >= count - count // 2**depth).astype(jnp.int32)
        return total

    levels = level(lax.broadcasted_iota(jnp.int32, (1, count), 1))
    mine = level(jnp.full((1, count), row, jnp.int32))
    two = (levels == 2).astype(F32)
    three_ = (levels == 3).astype(F32)
    one_mine = (mine == 1).astype(F32)
    two_mine = (mine == 2).astype(F32)
    late = (mine >= 2).astype(F32)
    use_row = line(weights * anc, row)
    above = line(anc, row)
    rows = [
        line(weights_t * anc_t, row) * (levels == 0).astype(F32),
        line(weights_t * anc, col),
        use_row * two * one_mine,
        use_row * three_ * (one_mine + two_mine),
        line(weights * anc_t, row) * late,
        above * two * one_mine,
        above * three_ * one_mine,
        above * three_ * two_mine,
        jnp.where(
            lax.broadcasted_iota(jnp.int32, (1, count), 1) == 0,
            (mine >= 1).astype(F32),
            (mine == 3).astype(F32),
        ),
        line(weights_t * anc, row) * one_mine,
    ]
    rows = rows + [jnp.zeros((1, count), F32)] * (out.shape[0] - len(rows))
    out[...] = jnp.concatenate(rows, 0)


def turn_kernel(block, out):
    out[...] = block[0, 0, 0, 0].astype(F32).T


def first_kernel(table, slices, y0, out, local_a, own_out):
    top, piece, width = slices.shape
    nrhs = y0.shape[1]
    half, quarter = top // 2, top // 4
    is_root = table[FLAGS, 1]
    own = slices[...].reshape(top * piece, width).astype(BF16)
    parts = jnp.concatenate(three(y0[...]), 1).astype(BF16)
    product = jnp.dot(own, parts, preferred_element_type=F32)
    product = product[:, :nrhs] + product[:, nrhs:2 * nrhs] + product[:, 2 * nrhs:]
    out[:top] = jnp.zeros((top, piece, nrhs), F32)
    out[top:] = product.reshape(top, piece, nrhs)
    for slot in range(quarter):
        total = (table[BELOW, top + half + slot] * is_root) * slices[half + slot]
        if slot < 2:
            line = (PICK_TWO, PICK_THREE)[slot]
            start = half + slot * quarter
            for k in range(start, start + quarter):
                total = total + table[line, top + k] * slices[k]
        local_a[0, slot] = total
    own_out[...] = own[:half * piece]


def leaf_kernel(table, got, out):
    total = table[FROM_LEAF, 0] * got[0]
    for k in range(1, got.shape[0] // 2):
        total = total + table[FROM_LEAF, k] * got[k]
    out[...] = total.T


def level_one_kernel(table, got, base_t, up, blocks, rest_out, y_out, out, held, arrived):
    copy = fetch(blocks, held, arrived, 0)
    pieces, rhs, piece = got.shape
    top = out.shape[0]
    width = base_t.shape[1]
    part = jnp.concatenate([got[k] for k in range(pieces)], 1)
    rest = base_t[...] - part * table[FLAGS, 0]
    y = mt(rest, up[...])
    rest_out[...] = rest
    y_out[...] = y
    copy.wait()
    a = mt(y, held[:, 0].reshape(width, width).astype(BF16))
    b = mt(y, held[:, 1].reshape(width, width).astype(BF16))
    for k in range(top):
        out[k] = table[SEND_TWO, top + k] * a + table[SEND_THREE, top + k] * b


def level_two_kernel(table, got, rest_in, up, blocks, rest_out, y_out, out, held, arrived):
    copy = fetch(blocks, held, arrived, 1)
    width = rest_in.shape[1]
    nz = out.shape[0]
    count = table.shape[1]
    rest = rest_in[...] - jnp.sum(got[...], 0)
    y = mt(rest, up[...])
    rest_out[...] = rest
    y_out[...] = y
    copy.wait()
    b = mt(y, held[:, 0].reshape(width, width).astype(BF16))
    for k in range(nz):
        out[k] = table[SEND_ROOT, count - nz + k] * b


def level_three_kernel(table, got, rest_in, up, low, blocks, y_out, out, held, arrived):
    copy = fetch(blocks, held, arrived, 0)
    width = rest_in.shape[1]
    nz = out.shape[0]
    slots = blocks.shape[1]
    rest = rest_in[...] - jnp.sum(got[...], 0)
    y = mt(rest, up[...])
    y_out[...] = y
    x = mt(y, low[...]) * table[FLAGS, 1]
    copy.wait()
    for k in range(slots):
        out[k] = mt(x, held[:, k].reshape(width, width).astype(BF16))
    for k in range(slots, nz):
        out[k] = jnp.zeros_like(x)


def level_two_back_kernel(got, y_in, low, out):
    out[0] = mt(y_in[...] - jnp.sum(got[...], 0), low[...])


def down_kernel(own, x, out):
    half, piece, nrhs = out.shape[0] // 2, out.shape[1], out.shape[2]
    parts = jnp.concatenate(three(x[...]), 0).astype(BF16)
    product = lax.dot_general(
        own[...], parts, (((1,), (1,)), ((), ())), preferred_element_type=F32
    )
    product = product[:, :nrhs] + product[:, nrhs:2 * nrhs] + product[:, 2 * nrhs:]
    out[:half] = product.reshape(half, piece, nrhs)
    out[half:] = jnp.zeros((half, piece, nrhs), F32)


def sum_kernel(table, got, out):
    top = got.shape[0]
    total = table[ABOVE, top + top // 2] * got[top // 2]
    for k in range(top // 2 + 1, top):
        total = total + table[ABOVE, top + k] * got[k]
    out[0] = total


def level_one_back_kernel(x, update, low, out):
    nrhs = update.shape[1]
    parts = jnp.concatenate(three(update[...]), 1).astype(BF16)
    product = jnp.dot(low[...], parts, preferred_element_type=F32)
    product = product[:, :nrhs] + product[:, nrhs:2 * nrhs] + product[:, 2 * nrhs:]
    out[...] = x[...].T - product


def a2a(array, axes):
    array = lax.optimization_barrier(array)
    return lax.optimization_barrier(lax.all_to_all(array, axes, 0, 0, tiled=True))


def copies(array, times):
    return jnp.broadcast_to(array[None], (times,) + array.shape)


def over_columns(array, ny):
    both = lax.all_gather(array, "core", tiled=True)
    return a2a(copies(both, ny), "y")


def per_device(factor, rhs, upper_inverse, lower_inverse, parents, block_mask):
    ny, nc, nz = lax.axis_size("y"), lax.axis_size("core"), lax.axis_size("z")
    ncol = ny * nc
    slot0 = factor[0, 0, 0, 0]
    base = rhs[0, 0]
    up = upper_inverse[0, 0]
    low = lower_inverse[0, 0]
    width, nrhs = base.shape
    piece = width // ncol
    mine = nrhs // ncol
    count = parents.shape[0]
    top = count // 2
    half, quarter = top // 2, top // 4
    small = width // count
    row = lax.axis_index(ROW)
    col = lax.axis_index(COL)
    is_high = lax.axis_index("xh") == 1

    sent = pl.pallas_call(
        turn_kernel,
        out_shape=shape_of(width, width),
        grid=(1,),
        in_specs=[pl.BlockSpec((1, 1, 1, 1, width, width), lambda k: (0, 0, 0, 1, 0, 0))],
        out_specs=pl.BlockSpec((width, width), lambda k: (0, 0)),
        compiler_params=ROOMY,
    )(factor).reshape(ncol, piece, width)
    table = call(
        table_kernel, shape_of(16, count), [SM, VM, VM, VM, VM],
        jnp.stack([row, col]).astype(jnp.int32), parents[None, :], parents[:, None],
        block_mask, block_mask.T,
    )
    y0 = jnp.dot(up.astype(F32), base, precision=HIGHEST)
    base_t = lax.dynamic_slice_in_dim(base.T, col * mine, mine, 0)

    slices = lax.all_to_all(sent, COL, 0, 0, tiled=True)
    table, y0, base_t, slices = lax.optimization_barrier((table, y0, base_t, slices))
    out, local_a, own = call(
        first_kernel,
        (
            shape_of(count, piece, nrhs),
            shape_of(1, quarter, piece, width),
            shape_of(half * piece, width, kind=BF16),
        ),
        [SM, VM, VM], table, slices, y0,
    )
    blocks_a = lax.all_gather(local_a, COL, tiled=True)

    part = call(leaf_kernel, shape_of(nrhs, piece), [SM, VM], table, a2a(out, ROW))
    got = a2a(part.reshape(ncol, mine, piece), COL)
    panel = shape_of(mine, width)
    rest, y, out = call(
        level_one_kernel, (panel, panel, shape_of(top, mine, width)), [SM, VM, VM, VM, HB],
        table, got, base_t, up, blocks_a, scratch=room(blocks_a, 2),
    )
    rest, y, out = call(
        level_two_kernel, (panel, panel, shape_of(nz, mine, width)), [SM, VM, VM, VM, HB],
        table, a2a(out, HALF), rest, up, blocks_a, scratch=room(blocks_a, 1),
    )
    y, out = call(
        level_three_kernel, (panel, shape_of(nz, mine, width)), [SM, VM, VM, VM, VM, HB],
        table, a2a(out, "z"), rest, up, low, blocks_a, scratch=room(blocks_a, quarter),
    )
    x = call(level_two_back_kernel, shape_of(1, mine, width), [VM, VM, VM], a2a(out, "z"), y, low)
    x = over_columns(x, ny).reshape(nrhs, width)
    out = call(down_kernel, shape_of(top, piece, nrhs), [VM, VM], own, x)
    part = call(sum_kernel, shape_of(1, piece, nrhs), [SM, VM], table, a2a(out, HALF))
    update = over_columns(part, ny).reshape(width, nrhs)
    x = call(level_one_back_kernel, shape_of(width, nrhs), [VM, VM, VM], x, update, low)
    full = lax.dot_general(
        slot0.astype(F32), x, (((0,), (0,)), ((), ())), precision=HIGHEST
    )
    got = a2a(full.reshape(count, small, nrhs), ROW)
    part = jnp.sum(table[FROM_LOW][:, None, None] * got, axis=0)
    every = over_columns(part[None], ny).reshape(ncol, small, nrhs)
    got = a2a(jnp.concatenate([every, jnp.zeros_like(every)], 0), ROW).reshape(width, nrhs)
    below = jnp.dot(low.astype(F32), y0 - got, precision=HIGHEST)
    return jnp.where(is_high, x, below)[None, None]


def solution(mesh):
    grid = Mesh(mesh.devices.reshape(2, 2, 8, 8, 2), ("xh", "xl", "z", "y", "core"))
    placed = (
        P(ROW, None, COL, None, None, None),
        P(ROW, None, None, None),
        P(ROW, None, None, None),
        P(ROW, None, None, None),
        P(),
        P(),
    )
    return jax.shard_map(
        per_device,
        mesh=grid,
        in_specs=placed,
        out_specs=P(ROW, None, None, None),
        check_vma=False,
    )
```

```python
import functools

import jax
import jax.numpy as jnp
from jax import lax
from jax.experimental import pallas as pl
from jax.experimental.pallas import tpu as pltpu
from jax.sharding import Mesh, PartitionSpec as P

LEVELS = 4
HALF = ("xl", "z")
ROW = ("xh", "xl", "z")
COL = ("y", "core")
ACROSS = ("xh", "y")
F32 = jnp.float32
BF16 = jnp.bfloat16
ROOMY = pltpu.CompilerParams(vmem_limit_bytes=40 * 1024 * 1024)
VM = pl.BlockSpec(memory_space=pltpu.VMEM)
SM = pl.BlockSpec(memory_space=pltpu.SMEM)

FROM_LEAF, FROM_ONE, FROM_TWO, FROM_THREE, FROM_ABOVE, TO_COLUMN, FLAGS = range(7)


def shape_of(*dims, kind=F32):
    return jax.ShapeDtypeStruct(dims, kind)


def call(body, shape, *args, scalars=0):
    out = [VM] * len(shape) if isinstance(shape, tuple) else VM
    return pl.pallas_call(
        body,
        out_shape=shape,
        in_specs=[SM] * scalars + [VM] * (len(args) - scalars),
        out_specs=out,
        compiler_params=ROOMY,
    )(*args)


def product(matrix, panel):
    cols = panel.shape[1]
    high = panel.astype(BF16).astype(F32)
    rest = panel - high
    mid = rest.astype(BF16).astype(F32)
    parts = jnp.concatenate([high, mid, rest - mid], 1).astype(BF16)
    full = jnp.dot(matrix, parts, preferred_element_type=F32)
    return full[:, :cols] + full[:, cols:2 * cols] + full[:, 2 * cols:]


def table_kernel(at, parents_row, parents_col, mask, mask_t, out):
    count = mask.shape[0]
    top = count // 2
    row, col = at[0], at[1]
    down = lax.broadcasted_iota(jnp.int32, (count, count), 0)
    across = lax.broadcasted_iota(jnp.int32, (count, count), 1)
    step = (parents_col[...] == across).astype(F32)
    step_t = (parents_row[...] == down).astype(F32)
    identity = (down == across).astype(F32)
    anc = power = anc_t = power_t = identity
    for _ in range(LEVELS - 1):
        power = jnp.dot(power, step, preferred_element_type=F32)
        power_t = jnp.dot(step_t, power_t, preferred_element_type=F32)
        anc = anc + power
        anc_t = anc_t + power_t
    anc = jnp.minimum(anc, 1.0)
    anc_t = jnp.minimum(anc_t, 1.0)
    weights_t = mask_t[...].astype(F32) * (1.0 - identity)
    upper_t = weights_t * anc_t
    lower_t = weights_t * anc

    def line(matrix, index):
        return jnp.sum(jnp.where(down == index, matrix, 0.0), axis=0, keepdims=True)

    def level(ids):
        total = jnp.zeros_like(ids)
        for depth in range(1, LEVELS):
            total = total + (ids >= count - count // 2**depth).astype(jnp.int32)
        return total

    levels = level(lax.broadcasted_iota(jnp.int32, (1, count), 1))
    mine = level(jnp.full((1, count), row, jnp.int32))
    low = (mine == 0).astype(F32)
    high = (mine >= 1).astype(F32)
    late = (mine >= 2).astype(F32)
    image = jnp.where(row < top, row + top, row)
    rows = [
        line(upper_t, image) * (levels == 0).astype(F32) * low,
        line(upper_t, row) * (levels == 1).astype(F32) * high,
        line(upper_t, row) * (levels == 2).astype(F32) * late,
        line(lower_t, row) * (levels == 3).astype(F32) * late,
        line(lower_t, row) * high,
        line(lower_t, col) * high,
        high,
    ]
    rows = rows + [jnp.zeros((1, count), F32)] * (out.shape[0] - len(rows))
    out[...] = jnp.concatenate(rows, 0)


def turn_kernel(block, out):
    turned = block[0, 0, 0, 0].astype(F32).T
    ncol, piece = out.shape[0], out.shape[1]
    ny = ncol // 2
    for y in range(ny):
        for core in range(2):
            start = (core * ny + y) * piece
            out[2 * y + core] = turned[start:start + piece]


def turn_whole_kernel(block, out):
    out[...] = block[0, 0, 0, 0].astype(F32).T.astype(BF16)


def slot_call(body, shape, factor, slot):
    width = factor.shape[-1]
    return pl.pallas_call(
        body,
        out_shape=shape,
        grid=(1,),
        in_specs=[pl.BlockSpec((1, 1, 1, 1, width, width), lambda k: (0, 0, 0, slot, 0, 0))],
        out_specs=pl.BlockSpec(shape.shape, lambda k: (0,) * len(shape.shape)),
        compiler_params=ROOMY,
    )(factor)


def leaf_kernel(slices, y0, out, own_out):
    top, piece, width = slices.shape
    own = slices[...].reshape(top * piece, width).astype(BF16)
    own_out[...] = own
    out[...] = product(own, y0[...]).reshape(out.shape)


def sum_kernel(line, first, table, got, out):
    total = table[line, first] * got[0]
    for k in range(1, got.shape[0]):
        total = total + table[line, first + k] * got[k]
    for k in range(out.shape[0]):
        out[k] = total


def sum_keep_kernel(line, first, table, got, out, part_out):
    sum_kernel(line, first, table, got, out)
    part_out[...] = out[0]


def sum_more_kernel(line, first, table, got, part, out):
    total = part[...]
    for k in range(got.shape[0]):
        total = total + table[line, first + k] * got[k]
    for k in range(out.shape[0]):
        out[k] = total


def one_kernel(update, base, up, own, rest_out, out):
    rest = base[...] - update[...]
    rest_out[...] = rest
    out[...] = product(own[...], product(up[...], rest)).reshape(out.shape)


def two_kernel(update, rest, up, own, out):
    rows = own.shape[0] // 2
    y = product(up[...], rest[...] - update[...])
    out[...] = product(own[rows:], y).reshape(out.shape)


def three_kernel(update, rest, up, low, own, y_out, out):
    rows = own.shape[0] // 2
    y = product(up[...], rest[...] - update[...])
    y_out[...] = y
    out[...] = product(own[rows:], product(low[...], y)).reshape(out.shape)


def two_back_kernel(update, y, low, own, out):
    x = product(low[...], y[...] - update[...])
    out[...] = product(own[...], x).reshape(out.shape)


def one_back_kernel(update, y, low, below, x_out, out):
    x = product(low[...], y[...] - update[...])
    x_out[...] = x
    out[...] = product(below[...], x).reshape(out.shape)


def order_kernel(got, out):
    ny = got.shape[1]
    for y in range(ny):
        for core in range(2):
            out[2 * y + core] = got[core, y]


def last_kernel(table, update, y0, low, x, out):
    leaf = product(low[...], y0[...] - update[...])
    out[0, 0] = jnp.where(table[FLAGS, 0] > 0.5, x[...], leaf)


def a2a(array, axes):
    array = lax.optimization_barrier(array)
    return lax.optimization_barrier(lax.all_to_all(array, axes, 0, 0, tiled=True))


def per_device(factor, rhs, upper_inverse, lower_inverse, parents, block_mask):
    ny, nz = lax.axis_size("y"), lax.axis_size("z")
    ncol = ny * lax.axis_size("core")
    base = rhs[0, 0]
    up = upper_inverse[0, 0]
    low = lower_inverse[0, 0]
    width, nrhs = base.shape
    piece = width // ncol
    count = parents.shape[0]
    top = count // 2
    late = count - nz
    row = lax.axis_index(ROW)
    col = lax.axis_index(COL)
    panel = shape_of(width, nrhs)
    slice_ = shape_of(piece, nrhs)
    copies = shape_of(ny, piece, nrhs)
    across = shape_of(2 * ny, piece, nrhs)
    to_top = shape_of(top, piece, nrhs)
    to_late = shape_of(nz, piece, nrhs)

    sent = slot_call(turn_kernel, shape_of(ncol, piece, width), factor, 1)
    below = slot_call(turn_whole_kernel, shape_of(width, width, kind=BF16), factor, 0)
    table = call(
        table_kernel, shape_of(8, count),
        jnp.stack([row, col]).astype(jnp.int32), parents[None, :], parents[:, None],
        block_mask, block_mask.T, scalars=1,
    )
    y0 = jnp.dot(up.astype(F32), base, precision=lax.Precision.HIGHEST)

    slices = lax.all_to_all(sent, COL, 0, 0, tiled=True)
    table, y0, base, up, low, below, slices = lax.optimization_barrier(
        (table, y0, base, up, low, below, slices)
    )

    def total(line, first, got, shape):
        return call(functools.partial(sum_kernel, line, first), shape, table, got, scalars=1)

    def whole(half):
        return lax.all_gather(half, "core", tiled=True).reshape(width, nrhs)

    def spread(copied):
        return whole(a2a(copied, "y"))

    out, own = call(leaf_kernel, (to_top, shape_of(width, width, kind=BF16)), slices, y0)
    got = total(FROM_LEAF, 0, a2a(out, HALF), across)
    update = whole(a2a(got, ACROSS)[:ny])
    rest, out = call(one_kernel, (panel, to_top), update, base, up, own)
    got, part = call(
        functools.partial(sum_keep_kernel, FROM_ONE, top), (copies, slice_),
        table, a2a(out, HALF), scalars=1,
    )
    out = call(two_kernel, to_late, spread(got), rest, up, own)
    got = call(
        functools.partial(sum_more_kernel, FROM_TWO, late), copies,
        table, a2a(out, "z"), part, scalars=1,
    )
    y, out = call(three_kernel, (panel, to_late), spread(got), rest, up, low, own)
    got = total(FROM_THREE, late, a2a(out, "z"), copies)
    out = call(two_back_kernel, to_top, spread(got), y, low, own)
    got = total(FROM_ABOVE, top, a2a(out, HALF), copies)
    x, out = call(one_back_kernel, (panel, to_top), spread(got), y, low, below)
    got = total(TO_COLUMN, top, a2a(out, HALF), across)
    got = a2a(got, ACROSS)[ny:]
    got = lax.all_gather(got, "core")
    out = call(order_kernel, to_top, got)
    update = a2a(out, HALF).reshape(width, nrhs)
    return call(
        last_kernel, shape_of(1, 1, width, nrhs), table, update, y0, low, x, scalars=1
    )


def solution(mesh):
    grid = Mesh(mesh.devices.reshape(2, 2, 8, 8, 2), ("xh", "xl", "z", "y", "core"))
    placed = (
        P(ROW, None, COL, None, None, None),
        P(ROW, None, None, None),
        P(ROW, None, None, None),
        P(ROW, None, None, None),
        P(),
        P(),
    )
    return jax.shard_map(
        per_device,
        mesh=grid,
        in_specs=placed,
        out_specs=P(ROW, None, None, None),
        check_vma=False,
    )
```

```python
import functools

import jax
import jax.numpy as jnp
from jax import lax
from jax.experimental import pallas as pl
from jax.experimental.pallas import tpu as pltpu
from jax.sharding import Mesh, PartitionSpec as P

LEVELS = 4
HALF = ("xl", "z")
ROW = ("xh", "xl", "z")
COL = ("y", "core")
ACROSS = ("xh", "y")
F32 = jnp.float32
BF16 = jnp.bfloat16
ROOMY = pltpu.CompilerParams(vmem_limit_bytes=40 * 1024 * 1024)
VM = pl.BlockSpec(memory_space=pltpu.VMEM)
SM = pl.BlockSpec(memory_space=pltpu.SMEM)

LEAF_COLUMN, FROM_ONE, FROM_TWO, FROM_THREE, FROM_ABOVE, TO_COLUMN, FLAGS = range(7)


def shape_of(*dims, kind=F32):
    return jax.ShapeDtypeStruct(dims, kind)


def call(body, shape, *args, scalars=0):
    out = [VM] * len(shape) if isinstance(shape, tuple) else VM
    return pl.pallas_call(
        body,
        out_shape=shape,
        in_specs=[SM] * scalars + [VM] * (len(args) - scalars),
        out_specs=out,
        compiler_params=ROOMY,
    )(*args)


def product(matrix, panel):
    cols = panel.shape[1]
    high = panel.astype(BF16).astype(F32)
    rest = panel - high
    mid = rest.astype(BF16).astype(F32)
    parts = jnp.concatenate([high, mid, rest - mid], 1).astype(BF16)
    full = jnp.dot(matrix, parts, preferred_element_type=F32)
    return full[:, :cols] + full[:, cols:2 * cols] + full[:, 2 * cols:]


def table_kernel(at, parents_row, parents_col, mask, mask_t, out):
    count = mask.shape[0]
    top = count // 2
    row, col = at[0], at[1]
    down = lax.broadcasted_iota(jnp.int32, (count, count), 0)
    across = lax.broadcasted_iota(jnp.int32, (count, count), 1)
    step = (parents_col[...] == across).astype(F32)
    step_t = (parents_row[...] == down).astype(F32)
    identity = (down == across).astype(F32)
    anc = power = anc_t = power_t = identity
    for _ in range(LEVELS - 1):
        power = jnp.dot(power, step, preferred_element_type=F32)
        power_t = jnp.dot(step_t, power_t, preferred_element_type=F32)
        anc = anc + power
        anc_t = anc_t + power_t
    anc = jnp.minimum(anc, 1.0)
    anc_t = jnp.minimum(anc_t, 1.0)
    weights_t = mask_t[...].astype(F32) * (1.0 - identity)
    upper_t = weights_t * anc_t
    lower_t = weights_t * anc

    def line(matrix, index):
        return jnp.sum(jnp.where(down == index, matrix, 0.0), axis=0, keepdims=True)

    def level(ids):
        total = jnp.zeros_like(ids)
        for depth in range(1, LEVELS):
            total = total + (ids >= count - count // 2**depth).astype(jnp.int32)
        return total

    levels = level(lax.broadcasted_iota(jnp.int32, (1, count), 1))
    mine = level(jnp.full((1, count), row, jnp.int32))
    low = (mine == 0).astype(F32)
    high = (mine >= 1).astype(F32)
    late = (mine >= 2).astype(F32)
    rows = [
        line(upper_t, top + col) * (levels == 0).astype(F32) * low,
        line(upper_t, row) * (levels == 1).astype(F32) * high,
        line(upper_t, row) * (levels == 2).astype(F32) * late,
        line(lower_t, row) * (levels == 3).astype(F32) * late,
        line(lower_t, row) * high,
        line(lower_t, col) * high,
        high,
    ]
    rows = rows + [jnp.zeros((1, count), F32)] * (out.shape[0] - len(rows))
    out[...] = jnp.concatenate(rows, 0)


def turn_kernel(at, block, whole, keep, send):
    rows = keep.shape[0]
    turned = block[0, 0, 0, 0].astype(F32).T
    whole[...] = turned.astype(BF16)
    mine = at[0] == 0
    keep[...] = jnp.where(mine, turned[:rows], turned[rows:])
    send[...] = jnp.where(mine, turned[rows:], turned[:rows])


def turn_whole_kernel(block, out):
    out[...] = block[0, 0, 0, 0].astype(F32).T.astype(BF16)


def parcel_kernel(at, own, other, *outs):
    ny = len(outs)
    piece = own.shape[0] // ny
    for step, out in enumerate(outs):
        start = pl.multiple_of(lax.rem(at[1] + step, ny) * piece, piece)
        out[:piece] = own[pl.ds(start, piece), :]
        out[piece:] = other[pl.ds(start, piece), :]


def unpack_kernel(at, *refs):
    parcels, out = refs[:-1], refs[-1]
    ny = len(parcels)
    piece = parcels[0].shape[0] // 2
    for step, parcel in enumerate(parcels):
        chip = 2 * lax.rem(at[1] + ny - step, ny)
        first = pl.multiple_of((chip + at[0]) * piece, piece)
        second = pl.multiple_of((chip + 1 - at[0]) * piece, piece)
        out[pl.ds(first, piece), :] = parcel[:piece].astype(BF16)
        out[pl.ds(second, piece), :] = parcel[piece:].astype(BF16)


def slot_call(body, shape, factor, slot):
    width = factor.shape[-1]
    return pl.pallas_call(
        body,
        out_shape=shape,
        grid=(1,),
        in_specs=[pl.BlockSpec((1, 1, 1, 1, width, width), lambda k: (0, 0, 0, slot, 0, 0))],
        out_specs=pl.BlockSpec(shape.shape, lambda k: (0,) * len(shape.shape)),
        compiler_params=ROOMY,
    )(factor)


def leaf_kernel(block, y0, out):
    out[...] = product(block[...], y0[...]).reshape(out.shape)


def sum_kernel(line, first, table, got, out):
    total = table[line, first] * got[0]
    for k in range(1, got.shape[0]):
        total = total + table[line, first + k] * got[k]
    for k in range(out.shape[0]):
        out[k] = total


def sum_keep_kernel(line, first, table, got, out, part_out):
    sum_kernel(line, first, table, got, out)
    part_out[...] = out[0]


def sum_more_kernel(line, first, table, got, part, out):
    total = part[...]
    for k in range(got.shape[0]):
        total = total + table[line, first + k] * got[k]
    for k in range(out.shape[0]):
        out[k] = total


def one_kernel(update, base, up, own, rest_out, out):
    rest = base[...] - update[...]
    rest_out[...] = rest
    out[...] = product(own[...], product(up[...], rest)).reshape(out.shape)


def two_kernel(update, rest, up, own, out):
    rows = own.shape[0] // 2
    y = product(up[...], rest[...] - update[...])
    out[...] = product(own[rows:], y).reshape(out.shape)


def three_kernel(update, rest, up, low, own, y_out, out):
    rows = own.shape[0] // 2
    y = product(up[...], rest[...] - update[...])
    y_out[...] = y
    out[...] = product(own[rows:], product(low[...], y)).reshape(out.shape)


def two_back_kernel(update, y, low, own, out):
    x = product(low[...], y[...] - update[...])
    out[...] = product(own[...], x).reshape(out.shape)


def one_back_kernel(update, y, low, below, x_out, out):
    x = product(low[...], y[...] - update[...])
    x_out[...] = x
    out[...] = product(below[...], x).reshape(out.shape)


def order_kernel(got, out):
    ny = got.shape[1]
    for y in range(ny):
        for core in range(2):
            out[2 * y + core] = got[core, y]


def last_kernel(table, update, y0, low, x, out):
    leaf = product(low[...], y0[...] - update[...])
    out[0, 0] = jnp.where(table[FLAGS, 0] > 0.5, x[...], leaf)


def a2a(array, axes):
    array = lax.optimization_barrier(array)
    return lax.optimization_barrier(lax.all_to_all(array, axes, 0, 0, tiled=True))


def per_device(factor, rhs, upper_inverse, lower_inverse, parents, block_mask):
    ny, nz = lax.axis_size("y"), lax.axis_size("z")
    ncol = ny * lax.axis_size("core")
    base = rhs[0, 0]
    up = upper_inverse[0, 0]
    low = lower_inverse[0, 0]
    width, nrhs = base.shape
    piece = width // ncol
    count = parents.shape[0]
    top = count // 2
    late = count - nz
    row = lax.axis_index(ROW)
    col = lax.axis_index(COL)
    panel = shape_of(width, nrhs)
    slice_ = shape_of(piece, nrhs)
    copies = shape_of(ny, piece, nrhs)
    across = shape_of(2 * ny, piece, nrhs)
    to_top = shape_of(top, piece, nrhs)
    to_late = shape_of(nz, piece, nrhs)

    at = jnp.stack([lax.axis_index("core"), lax.axis_index("y")]).astype(jnp.int32)
    half_block = shape_of(width // 2, width)
    turned, keep, send = pl.pallas_call(
        turn_kernel,
        out_shape=(shape_of(width, width, kind=BF16), half_block, half_block),
        grid=(1,),
        in_specs=[
            SM,
            pl.BlockSpec((1, 1, 1, 1, width, width), lambda k: (0, 0, 0, 1, 0, 0)),
        ],
        out_specs=(
            pl.BlockSpec((width, width), lambda k: (0, 0)),
            pl.BlockSpec((width // 2, width), lambda k: (0, 0)),
            pl.BlockSpec((width // 2, width), lambda k: (0, 0)),
        ),
        compiler_params=ROOMY,
    )(at, factor)
    below = slot_call(turn_whole_kernel, shape_of(width, width, kind=BF16), factor, 0)
    table = call(
        table_kernel, shape_of(8, count),
        jnp.stack([row, col]).astype(jnp.int32), parents[None, :], parents[:, None],
        block_mask, block_mask.T, scalars=1,
    )
    y0 = jnp.dot(up.astype(F32), base, precision=lax.Precision.HIGHEST)

    def shifted(parcel, step):
        return lax.ppermute(parcel, "y", [(k, (k + step) % ny) for k in range(ny)])

    def together(*arrays):
        return lax.optimization_barrier(arrays)

    def total(line, first, got, shape):
        return call(functools.partial(sum_kernel, line, first), shape, table, got, scalars=1)

    def whole(half):
        return lax.all_gather(half, "core", tiled=True).reshape(width, nrhs)

    def spread(copied):
        return whole(a2a(copied, "y"))

    out = call(leaf_kernel, to_top, turned, y0)
    out, send = together(out, send)
    other = lax.ppermute(send, "core", [(0, 1), (1, 0)])
    got = a2a(out, HALF)
    parcels = list(call(
        parcel_kernel, (shape_of(2 * piece, width),) * ny, at, keep, other, scalars=1
    ))
    got = total(LEAF_COLUMN, 0, got, across)
    got, parcels[1], parcels[7], parcels[2] = together(got, parcels[1], parcels[7], parcels[2])
    for step in (1, 7, 2):
        parcels[step] = shifted(parcels[step], step)
    got = lax.all_gather(a2a(got, ACROSS)[:ny], "core")
    out = call(order_kernel, to_top, got)
    out, parcels[6], parcels[3], parcels[5], parcels[4] = together(
        out, parcels[6], parcels[3], parcels[5], parcels[4]
    )
    for step in (6, 3, 5, 4):
        parcels[step] = shifted(parcels[step], step)
    update = a2a(out, HALF).reshape(width, nrhs)
    own = call(unpack_kernel, shape_of(width, width, kind=BF16), at, *parcels, scalars=1)
    rest, out = call(one_kernel, (panel, to_top), update, base, up, own)
    got, part = call(
        functools.partial(sum_keep_kernel, FROM_ONE, top), (copies, slice_),
        table, a2a(out, HALF), scalars=1,
    )
    out = call(two_kernel, to_late, spread(got), rest, up, own)
    got = call(
        functools.partial(sum_more_kernel, FROM_TWO, late), copies,
        table, a2a(out, "z"), part, scalars=1,
    )
    y, out = call(three_kernel, (panel, to_late), spread(got), rest, up, low, own)
    got = total(FROM_THREE, late, a2a(out, "z"), copies)
    out = call(two_back_kernel, to_top, spread(got), y, low, own)
    got = total(FROM_ABOVE, top, a2a(out, HALF), copies)
    x, out = call(one_back_kernel, (panel, to_top), spread(got), y, low, below)
    got = total(TO_COLUMN, top, a2a(out, HALF), across)
    got = a2a(got, ACROSS)[ny:]
    got = lax.all_gather(got, "core")
    out = call(order_kernel, to_top, got)
    update = a2a(out, HALF).reshape(width, nrhs)
    return call(
        last_kernel, shape_of(1, 1, width, nrhs), table, update, y0, low, x, scalars=1
    )


def solution(mesh):
    grid = Mesh(mesh.devices.reshape(2, 2, 8, 8, 2), ("xh", "xl", "z", "y", "core"))
    placed = (
        P(ROW, None, COL, None, None, None),
        P(ROW, None, None, None),
        P(ROW, None, None, None),
        P(ROW, None, None, None),
        P(),
        P(),
    )
    return jax.shard_map(
        per_device,
        mesh=grid,
        in_specs=placed,
        out_specs=P(ROW, None, None, None),
        check_vma=False,
    )
```

```python
import functools

import jax
import jax.numpy as jnp
from jax import lax
from jax.experimental import pallas as pl
from jax.experimental.pallas import tpu as pltpu
from jax.sharding import Mesh, PartitionSpec as P

LEVELS = 4
HALF = ("xl", "z")
ROW = ("xh", "xl", "z")
COL = ("y", "core")
ACROSS = ("xh", "y")
BESIDE = ("xl", "y")
F32 = jnp.float32
BF16 = jnp.bfloat16
ROOMY = pltpu.CompilerParams(vmem_limit_bytes=40 * 1024 * 1024)
VM = pl.BlockSpec(memory_space=pltpu.VMEM)
SM = pl.BlockSpec(memory_space=pltpu.SMEM)

FROM_LEAF, FROM_ONE, FROM_TWO, FROM_THREE, FROM_ABOVE, TO_COLUMN, FLAGS = range(7)


def shape_of(*dims, kind=F32):
    return jax.ShapeDtypeStruct(dims, kind)


def call(body, shape, *args, scalars=0):
    out = [VM] * len(shape) if isinstance(shape, tuple) else VM
    return pl.pallas_call(
        body,
        out_shape=shape,
        in_specs=[SM] * scalars + [VM] * (len(args) - scalars),
        out_specs=out,
        compiler_params=ROOMY,
    )(*args)


def product(matrix, panel):
    cols = panel.shape[1]
    high = panel.astype(BF16).astype(F32)
    rest = panel - high
    mid = rest.astype(BF16).astype(F32)
    parts = jnp.concatenate([high, mid, rest - mid], 1).astype(BF16)
    full = jnp.dot(matrix, parts, preferred_element_type=F32)
    return full[:, :cols] + full[:, cols:2 * cols] + full[:, 2 * cols:]


def table_kernel(at, parents_row, parents_col, mask, mask_t, out):
    count = mask.shape[0]
    top = count // 2
    row, col = at[0], at[1]
    down = lax.broadcasted_iota(jnp.int32, (count, count), 0)
    across = lax.broadcasted_iota(jnp.int32, (count, count), 1)
    step = (parents_col[...] == across).astype(F32)
    step_t = (parents_row[...] == down).astype(F32)
    identity = (down == across).astype(F32)
    anc = power = anc_t = power_t = identity
    for _ in range(LEVELS - 1):
        power = jnp.dot(power, step, preferred_element_type=F32)
        power_t = jnp.dot(step_t, power_t, preferred_element_type=F32)
        anc = anc + power
        anc_t = anc_t + power_t
    anc = jnp.minimum(anc, 1.0)
    anc_t = jnp.minimum(anc_t, 1.0)
    weights_t = mask_t[...].astype(F32) * (1.0 - identity)
    upper_t = weights_t * anc_t
    lower_t = weights_t * anc

    def line(matrix, index):
        return jnp.sum(jnp.where(down == index, matrix, 0.0), axis=0, keepdims=True)

    def level(ids):
        total = jnp.zeros_like(ids)
        for depth in range(1, LEVELS):
            total = total + (ids >= count - count // 2**depth).astype(jnp.int32)
        return total

    levels = level(lax.broadcasted_iota(jnp.int32, (1, count), 1))
    mine = level(jnp.full((1, count), row, jnp.int32))
    low = (mine == 0).astype(F32)
    high = (mine >= 1).astype(F32)
    late = (mine >= 2).astype(F32)
    image = jnp.where(row < top, row + top, row)
    one = high - late
    below_late = row + jnp.where(row < count - top // 2, top // 2, 0)
    above_one = row - jnp.where(row >= count - top // 2, top // 2, 0)
    flags = lax.broadcasted_iota(jnp.int32, (1, count), 1)
    rows = [
        line(upper_t, image) * (levels == 0).astype(F32) * low,
        line(upper_t, below_late) * (levels == 1).astype(F32) * high,
        line(upper_t, row) * (levels == 2).astype(F32) * late,
        line(lower_t, row) * (levels == 3).astype(F32) * late,
        line(lower_t, above_one) * high,
        line(lower_t, col) * high,
        jnp.where(flags == 0, high, jnp.where(flags == 1, late, one)),
    ]
    rows = rows + [jnp.zeros((1, count), F32)] * (out.shape[0] - len(rows))
    out[...] = jnp.concatenate(rows, 0)


def turn_kernel(blocks, out, block, turned, arrived, gone):
    copy = pltpu.make_async_copy(blocks.at[0, 0, 0, 1], block, arrived)
    copy.start()
    copy.wait()
    whole = block[...].astype(F32).T
    ncol, piece = turned.shape[0], turned.shape[1]
    ny = ncol // 2
    for y in range(ny):
        for core in range(2):
            start = (core * ny + y) * piece
            turned[2 * y + core] = whole[start:start + piece]
    copy = pltpu.make_async_copy(turned, out, gone)
    copy.start()
    copy.wait()


def turn_whole_kernel(blocks, out, block, arrived):
    copy = pltpu.make_async_copy(blocks.at[0, 0, 0, 0], block, arrived)
    copy.start()
    copy.wait()
    out[...] = block[...].astype(F32).T.astype(BF16)


def slot_call(body, shape, factor, space, scratch):
    width = factor.shape[-1]
    return pl.pallas_call(
        body,
        out_shape=shape,
        in_specs=[pl.BlockSpec(memory_space=pltpu.HBM)],
        out_specs=pl.BlockSpec(memory_space=space),
        scratch_shapes=[pltpu.VMEM((width, width), BF16)] + scratch,
        compiler_params=ROOMY,
    )(factor)


def leaf_kernel(slices, y0, out, own_out):
    top, piece, width = slices.shape
    own = slices[...].reshape(top * piece, width).astype(BF16)
    own_out[...] = own
    out[...] = product(own, y0[...]).reshape(out.shape)


def sum_kernel(line, first, table, got, out):
    total = table[line, first] * got[0]
    for k in range(1, got.shape[0]):
        total = total + table[line, first + k] * got[k]
    for k in range(out.shape[0]):
        out[k] = total


def halves(out, panel, piece):
    slices = panel.reshape(panel.shape[0] // piece, piece, panel.shape[1])
    count = slices.shape[0]
    out[:count] = slices[:, :piece // 2]
    out[count:] = slices[:, piece // 2:]


def joined(update):
    cores, parts, ny = update.shape[:3]
    return jnp.concatenate(
        [
            update[core, part, y]
            for core in range(cores)
            for y in range(ny)
            for part in range(parts)
        ],
        0,
    )


def one_kernel(update, base, up, own, rest_out, out):
    rows = own.shape[0] // 2
    rest = base[...] - update[...]
    rest_out[...] = rest
    halves(out, product(own[rows:], product(up[...], rest)), 2 * out.shape[1])


def two_kernel(table, update, rest_in, up, own, rest_out, out):
    rows = own.shape[0] // 2
    rest = rest_in[...] - joined(update) * table[FLAGS, 1]
    rest_out[...] = rest
    out[...] = product(own[rows:], product(up[...], rest)).reshape(out.shape)


def three_kernel(update, rest, up, low, own, y_out, out):
    rows = own.shape[0] // 2
    y = product(up[...], rest[...] - update[...])
    y_out[...] = y
    out[...] = product(own[rows:], product(low[...], y)).reshape(out.shape)


def two_back_kernel(update, y, low, own, rest_out, out):
    rows = own.shape[0] // 2
    rest = y[...] - update[...]
    rest_out[...] = rest
    halves(out, product(own[:rows], product(low[...], rest)), 2 * out.shape[1])


def one_back_kernel(table, update, rest, low, below, x_out, out):
    x = product(low[...], rest[...] - joined(update) * table[FLAGS, 2])
    x_out[...] = x
    out[...] = product(below[...], x).reshape(out.shape)


def order_kernel(got, out):
    ny = got.shape[1]
    for y in range(ny):
        for core in range(2):
            out[2 * y + core] = got[core, y]


def last_kernel(table, update, y0, low, x, out):
    leaf = product(low[...], y0[...] - update[...])
    out[0, 0] = jnp.where(table[FLAGS, 0] > 0.5, x[...], leaf)


def a2a(array, axes):
    array = lax.optimization_barrier(array)
    return lax.optimization_barrier(lax.all_to_all(array, axes, 0, 0, tiled=True))


def per_device(factor, rhs, upper_inverse, lower_inverse, parents, block_mask):
    ny, nz = lax.axis_size("y"), lax.axis_size("z")
    ncol = ny * lax.axis_size("core")
    base = rhs[0, 0]
    up = upper_inverse[0, 0]
    low = lower_inverse[0, 0]
    width, nrhs = base.shape
    piece = width // ncol
    count = parents.shape[0]
    top = count // 2
    late = count - nz
    row = lax.axis_index(ROW)
    col = lax.axis_index(COL)
    panel = shape_of(width, nrhs)
    half_to_top = shape_of(top, piece // 2, nrhs)
    copies = shape_of(ny, piece, nrhs)
    across = shape_of(2 * ny, piece, nrhs)
    to_top = shape_of(top, piece, nrhs)
    to_late = shape_of(nz, piece, nrhs)

    sent = slot_call(
        turn_kernel, shape_of(ncol, piece, width), factor, pltpu.HBM,
        [pltpu.VMEM((ncol, piece, width), F32), pltpu.SemaphoreType.DMA, pltpu.SemaphoreType.DMA],
    )
    below = slot_call(
        turn_whole_kernel, shape_of(width, width, kind=BF16), factor, pltpu.VMEM,
        [pltpu.SemaphoreType.DMA],
    )
    table = call(
        table_kernel, shape_of(8, count),
        jnp.stack([row, col]).astype(jnp.int32), parents[None, :], parents[:, None],
        block_mask, block_mask.T, scalars=1,
    )
    y0 = jnp.dot(up.astype(F32), base, precision=lax.Precision.HIGHEST)

    slices = lax.all_to_all(sent, COL, 0, 0, tiled=True)
    table, y0, base, up, low, below, slices = lax.optimization_barrier(
        (table, y0, base, up, low, below, slices)
    )

    def total(line, first, got, shape):
        return call(functools.partial(sum_kernel, line, first), shape, table, got, scalars=1)

    def whole(half):
        return lax.all_gather(half, "core", tiled=True).reshape(width, nrhs)

    def spread(copied):
        return whole(a2a(copied, "y"))

    def spread_halves(copied):
        both = lax.all_gather(a2a(copied, BESIDE), "core", tiled=True)
        return both.reshape(ncol // ny, 2, ny, piece // 2, nrhs)

    out, own = call(leaf_kernel, (to_top, shape_of(width, width, kind=BF16)), slices, y0)
    got = total(FROM_LEAF, 0, a2a(out, HALF), across)
    update = whole(a2a(got, ACROSS)[:ny])
    rest, out = call(one_kernel, (panel, half_to_top), update, base, up, own)
    got = total(FROM_ONE, top, a2a(out, HALF), half_to_top)
    rest, out = call(
        two_kernel, (panel, to_late), table, spread_halves(got), rest, up, own, scalars=1
    )
    got = total(FROM_TWO, late, a2a(out, "z"), copies)
    y, out = call(three_kernel, (panel, to_late), spread(got), rest, up, low, own)
    got = total(FROM_THREE, late, a2a(out, "z"), copies)
    rest, out = call(two_back_kernel, (panel, half_to_top), spread(got), y, low, own)
    got = total(FROM_ABOVE, top, a2a(out, HALF), half_to_top)
    x, out = call(
        one_back_kernel, (panel, to_top), table, spread_halves(got), rest, low, below, scalars=1
    )
    got = total(TO_COLUMN, top, a2a(out, HALF), across)
    got = a2a(got, ACROSS)[ny:]
    got = lax.all_gather(got, "core")
    out = call(order_kernel, to_top, got)
    update = a2a(out, HALF).reshape(width, nrhs)
    return call(
        last_kernel, shape_of(1, 1, width, nrhs), table, update, y0, low, x, scalars=1
    )


def solution(mesh):
    grid = Mesh(mesh.devices.reshape(2, 2, 8, 8, 2), ("xh", "xl", "z", "y", "core"))
    placed = (
        P(ROW, None, COL, None, None, None),
        P(ROW, None, None, None),
        P(ROW, None, None, None),
        P(ROW, None, None, None),
        P(),
        P(),
    )
    return jax.shard_map(
        per_device,
        mesh=grid,
        in_specs=placed,
        out_specs=P(ROW, None, None, None),
        check_vma=False,
    )
```

```python
import functools

import jax
import jax.numpy as jnp
from jax import lax
from jax.experimental import pallas as pl
from jax.experimental.pallas import tpu as pltpu
from jax.sharding import Mesh, PartitionSpec as P

LEVELS = 4
HALF = ("xl", "z")
ROW = ("xh", "xl", "z")
COL = ("y", "core")
ACROSS = ("xh", "y")
BESIDE = ("xl", "y")
F32 = jnp.float32
BF16 = jnp.bfloat16
ROOMY = pltpu.CompilerParams(vmem_limit_bytes=40 * 1024 * 1024)
VM = pl.BlockSpec(memory_space=pltpu.VMEM)
SM = pl.BlockSpec(memory_space=pltpu.SMEM)

FROM_LEAF, FROM_ONE, FROM_TWO, FROM_THREE, FROM_ABOVE, TO_COLUMN, HIGH = range(7)


def shape_of(*dims, kind=F32):
    return jax.ShapeDtypeStruct(dims, kind)


def call(body, shape, *args, scalars=0):
    out = [VM] * len(shape) if isinstance(shape, tuple) else VM
    return pl.pallas_call(
        body,
        out_shape=shape,
        in_specs=[SM] * scalars + [VM] * (len(args) - scalars),
        out_specs=out,
        compiler_params=ROOMY,
    )(*args)


def product(matrix, panel):
    cols = panel.shape[1]
    high = panel.astype(BF16).astype(F32)
    rest = panel - high
    mid = rest.astype(BF16).astype(F32)
    parts = jnp.concatenate([high, mid, rest - mid], 1).astype(BF16)
    full = jnp.dot(matrix, parts, preferred_element_type=F32)
    return full[:, :cols] + full[:, cols:2 * cols] + full[:, 2 * cols:]


def table_kernel(at, parents_row, parents_col, mask, out):
    count = mask.shape[0]
    top = count // 2
    row, col = at[0], at[1]
    down = lax.broadcasted_iota(jnp.int32, (count, count), 0)
    across = lax.broadcasted_iota(jnp.int32, (count, count), 1)
    step = (parents_col[...] == across).astype(F32)
    step_t = (parents_row[...] == down).astype(F32)
    identity = (down == across).astype(F32)
    anc = power = anc_t = power_t = identity
    for _ in range(LEVELS - 1):
        power = jnp.dot(power, step, preferred_element_type=F32)
        power_t = jnp.dot(step_t, power_t, preferred_element_type=F32)
        anc = anc + power
        anc_t = anc_t + power_t
    weights = mask[...].astype(F32) * (1.0 - identity)
    upper = weights * jnp.minimum(anc, 1.0)
    lower = weights * jnp.minimum(anc_t, 1.0)

    def column(matrix, index):
        return jnp.sum(jnp.where(across == index, matrix, 0.0), axis=1, keepdims=True)

    def level(ids):
        total = jnp.zeros_like(ids)
        for depth in range(1, LEVELS):
            total = total + (ids >= count - count // 2**depth).astype(jnp.int32)
        return total

    levels = level(lax.broadcasted_iota(jnp.int32, (count, 1), 0))
    mine = level(jnp.full((count, 1), row, jnp.int32))
    low = (mine == 0).astype(F32)
    high = (mine >= 1).astype(F32)
    late = (mine >= 2).astype(F32)
    image = jnp.where(row < top, row + top, row)
    below_late = row + jnp.where(row < count - top // 2, top // 2, 0)
    above_one = row - jnp.where(row >= count - top // 2, top // 2, 0)
    lines = [
        column(upper, image) * (levels == 0).astype(F32) * low,
        column(upper, below_late) * (levels == 1).astype(F32) * high,
        column(upper, row) * (levels == 2).astype(F32) * late,
        column(lower, row) * (levels == 3).astype(F32) * late,
        column(lower, above_one) * high,
        column(lower, col) * high,
        high,
    ]
    for index, values in enumerate(lines):
        out[index] = jnp.broadcast_to(values, (count, out.shape[2]))


def turn_kernel(blocks, out, block, turned, arrived, gone):
    copy = pltpu.make_async_copy(blocks.at[0, 0, 0, 1], block, arrived)
    copy.start()
    copy.wait()
    whole = block[...].astype(F32).T
    ncol, piece = turned.shape[0], turned.shape[1]
    ny = ncol // 2
    for y in range(ny):
        for core in range(2):
            start = (core * ny + y) * piece
            turned[2 * y + core] = whole[start:start + piece]
    copy = pltpu.make_async_copy(turned, out, gone)
    copy.start()
    copy.wait()


def turn_whole_kernel(blocks, out, block, arrived):
    copy = pltpu.make_async_copy(blocks.at[0, 0, 0, 0], block, arrived)
    copy.start()
    copy.wait()
    out[...] = block[...].astype(F32).T.astype(BF16)


def slot_call(body, shape, factor, space, scratch):
    width = factor.shape[-1]
    return pl.pallas_call(
        body,
        out_shape=shape,
        in_specs=[pl.BlockSpec(memory_space=pltpu.HBM)],
        out_specs=pl.BlockSpec(memory_space=space),
        scratch_shapes=[pltpu.VMEM((width, width), BF16)] + scratch,
        compiler_params=pltpu.CompilerParams(vmem_limit_bytes=60 * 1024 * 1024),
    )(factor)


def leaf_kernel(slices, y0, out, own_out):
    top, piece, width = slices.shape
    own = slices[...].reshape(top * piece, width).astype(BF16)
    own_out[...] = own
    out[...] = product(own, y0[...]).reshape(out.shape)


def sum_kernel(line, first, start, stop, table, got, out):
    total = table[line, first:first + 1] * got[0]
    for k in range(1, got.shape[0]):
        total = total + table[line, first + k:first + k + 1] * got[k]
    for k in range(out.shape[0]):
        out[k] = total if start <= k < stop else jnp.zeros_like(total)


def halves(out, panel, piece):
    slices = panel.reshape(panel.shape[0] // piece, piece, panel.shape[1])
    count = slices.shape[0]
    out[:count] = slices[:, :piece // 2]
    out[count:] = slices[:, piece // 2:]


def joined(update):
    cores, parts, ny = update.shape[:3]
    return jnp.concatenate(
        [
            update[core, part, y]
            for core in range(cores)
            for y in range(ny)
            for part in range(parts)
        ],
        0,
    )


def one_kernel(update, base, up, own, rest_out, out):
    rows = own.shape[0] // 2
    rest = base[...] - update[...]
    rest_out[...] = rest
    halves(out, product(own[rows:], product(up[...], rest)), 2 * out.shape[1])


def two_kernel(update, rest_in, up, own, rest_out, out):
    rows = own.shape[0] // 2
    rest = rest_in[...] - joined(update)
    rest_out[...] = rest
    out[...] = product(own[rows:], product(up[...], rest)).reshape(out.shape)


def three_kernel(update, rest, up, low, own, y_out, out):
    rows = own.shape[0] // 2
    y = product(up[...], rest[...] - update[...])
    y_out[...] = y
    out[...] = product(own[rows:], product(low[...], y)).reshape(out.shape)


def two_back_kernel(update, y, low, own, rest_out, out):
    rows = own.shape[0] // 2
    rest = y[...] - update[...]
    rest_out[...] = rest
    halves(out, product(own[:rows], product(low[...], rest)), 2 * out.shape[1])


def one_back_kernel(update, rest, low, below, x_out, out):
    x = product(low[...], rest[...] - joined(update))
    x_out[...] = x
    out[...] = product(below[...], x).reshape(out.shape)


def order_kernel(got, out):
    ny = got.shape[1]
    for y in range(ny):
        for core in range(2):
            out[2 * y + core] = got[core, y]


def last_kernel(table, update, y0, low, x, out):
    leaf = product(low[...], y0[...] - update[...])
    out[0, 0] = jnp.where(table[HIGH, 0:1] > 0.5, x[...], leaf)


def a2a(array, axes):
    array = lax.optimization_barrier(array)
    return lax.optimization_barrier(lax.all_to_all(array, axes, 0, 0, tiled=True))


def per_device(factor, rhs, upper_inverse, lower_inverse, parents, block_mask):
    ny, nz = lax.axis_size("y"), lax.axis_size("z")
    ncol = ny * lax.axis_size("core")
    base = rhs[0, 0]
    up = upper_inverse[0, 0]
    low = lower_inverse[0, 0]
    width, nrhs = base.shape
    piece = width // ncol
    count = parents.shape[0]
    top = count // 2
    late = count - nz
    row = lax.axis_index(ROW)
    col = lax.axis_index(COL)
    panel = shape_of(width, nrhs)
    half_to_top = shape_of(top, piece // 2, nrhs)
    copies = shape_of(ny, piece, nrhs)
    across = shape_of(2 * ny, piece, nrhs)
    to_top = shape_of(top, piece, nrhs)
    to_late = shape_of(nz, piece, nrhs)

    sent = slot_call(
        turn_kernel, shape_of(ncol, piece, width), factor, pltpu.HBM,
        [pltpu.VMEM((ncol, piece, width), F32), pltpu.SemaphoreType.DMA, pltpu.SemaphoreType.DMA],
    )
    below = slot_call(
        turn_whole_kernel, shape_of(width, width, kind=BF16), factor, pltpu.VMEM,
        [pltpu.SemaphoreType.DMA],
    )
    table = call(
        table_kernel, shape_of(HIGH + 1, count, nrhs),
        jnp.stack([row, col]).astype(jnp.int32), parents[None, :], parents[:, None],
        block_mask, scalars=1,
    )
    y0 = jnp.dot(up.astype(F32), base, precision=lax.Precision.HIGHEST)

    slices = lax.all_to_all(sent, COL, 0, 0, tiled=True)
    table, y0, base, up, low, below, slices = lax.optimization_barrier(
        (table, y0, base, up, low, below, slices)
    )

    def total(line, first, got, shape, start=0, stop=ncol):
        body = functools.partial(sum_kernel, line, first, start, stop)
        return call(body, shape, table, got)

    def whole(half):
        return lax.all_gather(half, "core", tiled=True).reshape(width, nrhs)

    def spread(copied):
        return whole(a2a(copied, "y"))

    def spread_halves(copied):
        both = lax.all_gather(a2a(copied, BESIDE), "core", tiled=True)
        return both.reshape(ncol // ny, 2, ny, piece // 2, nrhs)

    out, own = call(leaf_kernel, (to_top, shape_of(width, width, kind=BF16)), slices, y0)
    got = total(FROM_LEAF, 0, a2a(out, HALF), across, start=ny)
    update = whole(a2a(got, ACROSS)[:ny])
    rest, out = call(one_kernel, (panel, half_to_top), update, base, up, own)
    got = total(FROM_ONE, top, a2a(out, HALF), half_to_top, start=ny)
    rest, out = call(
        two_kernel, (panel, to_late), spread_halves(got), rest, up, own
    )
    got = total(FROM_TWO, late, a2a(out, "z"), copies)
    y, out = call(three_kernel, (panel, to_late), spread(got), rest, up, low, own)
    got = total(FROM_THREE, late, a2a(out, "z"), copies)
    rest, out = call(two_back_kernel, (panel, half_to_top), spread(got), y, low, own)
    got = total(FROM_ABOVE, top, a2a(out, HALF), half_to_top, stop=ny)
    x, out = call(
        one_back_kernel, (panel, to_top), spread_halves(got), rest, low, below
    )
    got = total(TO_COLUMN, top, a2a(out, HALF), across, stop=ny)
    got = a2a(got, ACROSS)[ny:]
    got = lax.all_gather(got, "core")
    out = call(order_kernel, to_top, got)
    update = a2a(out, HALF).reshape(width, nrhs)
    return call(
        last_kernel, shape_of(1, 1, width, nrhs), table, update, y0, low, x
    )


def solution(mesh):
    grid = Mesh(mesh.devices.reshape(2, 2, 8, 8, 2), ("xh", "xl", "z", "y", "core"))
    placed = (
        P(ROW, None, COL, None, None, None),
        P(ROW, None, None, None),
        P(ROW, None, None, None),
        P(ROW, None, None, None),
        P(),
        P(),
    )
    return jax.shard_map(
        per_device,
        mesh=grid,
        in_specs=placed,
        out_specs=P(ROW, None, None, None),
        check_vma=False,
    )
```

```python
import functools

import jax
import jax.numpy as jnp
from jax import lax
from jax.experimental import pallas as pl
from jax.experimental.pallas import tpu as pltpu
from jax.sharding import Mesh, PartitionSpec as P

LEVELS = 4
HALF = ("xl", "z")
ROW = ("xh", "xl", "z")
COL = ("y", "core")
ACROSS = ("xh", "y")
BESIDE = ("xl", "y")
F32 = jnp.float32
BF16 = jnp.bfloat16
ROOMY = pltpu.CompilerParams(vmem_limit_bytes=40 * 1024 * 1024)
VM = pl.BlockSpec(memory_space=pltpu.VMEM)
SM = pl.BlockSpec(memory_space=pltpu.SMEM)

FROM_LEAF, FROM_ONE, FROM_TWO, FROM_THREE, FROM_ABOVE, TO_COLUMN, HIGH = range(7)


def shape_of(*dims, kind=F32):
    return jax.ShapeDtypeStruct(dims, kind)


def call(body, shape, *args, scalars=0):
    out = [VM] * len(shape) if isinstance(shape, tuple) else VM
    return pl.pallas_call(
        body,
        out_shape=shape,
        in_specs=[SM] * scalars + [VM] * (len(args) - scalars),
        out_specs=out,
        compiler_params=ROOMY,
    )(*args)


def product(matrix, panel):
    cols = panel.shape[1]
    high = panel.astype(BF16).astype(F32)
    rest = panel - high
    mid = rest.astype(BF16).astype(F32)
    parts = jnp.concatenate([high, mid, rest - mid], 1).astype(BF16)
    full = jnp.dot(matrix, parts, preferred_element_type=F32)
    return full[:, :cols] + full[:, cols:2 * cols] + full[:, 2 * cols:]


def table_kernel(at, parents_row, parents_col, mask, out):
    count = mask.shape[0]
    top = count // 2
    row, col = at[0], at[1]
    down = lax.broadcasted_iota(jnp.int32, (count, count), 0)
    across = lax.broadcasted_iota(jnp.int32, (count, count), 1)
    step = (parents_col[...] == across).astype(F32)
    step_t = (parents_row[...] == down).astype(F32)
    identity = (down == across).astype(F32)
    anc = power = anc_t = power_t = identity
    for _ in range(LEVELS - 1):
        power = jnp.dot(power, step, preferred_element_type=F32)
        power_t = jnp.dot(step_t, power_t, preferred_element_type=F32)
        anc = anc + power
        anc_t = anc_t + power_t
    weights = mask[...].astype(F32) * (1.0 - identity)
    upper = weights * jnp.minimum(anc, 1.0)
    lower = weights * jnp.minimum(anc_t, 1.0)

    def column(matrix, index):
        return jnp.sum(jnp.where(across == index, matrix, 0.0), axis=1, keepdims=True)

    def level(ids):
        total = jnp.zeros_like(ids)
        for depth in range(1, LEVELS):
            total = total + (ids >= count - count // 2**depth).astype(jnp.int32)
        return total

    levels = level(lax.broadcasted_iota(jnp.int32, (count, 1), 0))
    mine = level(jnp.full((count, 1), row, jnp.int32))
    low = (mine == 0).astype(F32)
    high = (mine >= 1).astype(F32)
    late = (mine >= 2).astype(F32)
    image = jnp.where(row < top, row + top, row)
    below_late = row + jnp.where(row < count - top // 2, top // 2, 0)
    above_one = row - jnp.where(row >= count - top // 2, top // 2, 0)
    lines = [
        column(upper, image) * (levels == 0).astype(F32) * low,
        column(upper, below_late) * (levels == 1).astype(F32) * high,
        column(upper, row) * (levels == 2).astype(F32) * late,
        column(lower, row) * (levels == 3).astype(F32) * late,
        column(lower, above_one) * high,
        column(lower, col) * high,
        high,
    ]
    for index, values in enumerate(lines):
        out[index] = jnp.broadcast_to(values, (count, out.shape[2]))


def turn_kernel(blocks, out, block, turned, arrived, gone):
    ncol, piece = turned.shape[0], turned.shape[1]
    ny = ncol // 2
    part = 128
    inward = []
    for k in range(block.shape[1] // part):
        lanes = pl.ds(k * part, part)
        copy = pltpu.make_async_copy(
            blocks.at[0, 0, 0, 1, :, lanes], block.at[:, lanes], arrived.at[k]
        )
        copy.start()
        inward.append(copy)
    outward = []
    for k, copy in enumerate(inward):
        copy.wait()
        rows = block[:, k * part:(k + 1) * part].astype(F32).T
        for j in range(part // piece):
            core, y = divmod(k * (part // piece) + j, ny)
            to = 2 * y + core
            turned[to] = rows[j * piece:(j + 1) * piece]
            copy = pltpu.make_async_copy(turned.at[to], out.at[to], gone.at[to])
            copy.start()
            outward.append(copy)
    for copy in outward:
        copy.wait()


def turn_whole_kernel(blocks, out, block, arrived):
    copy = pltpu.make_async_copy(blocks.at[0, 0, 0, 0], block, arrived)
    copy.start()
    copy.wait()
    out[...] = block[...].astype(F32).T.astype(BF16)


def slot_call(body, shape, factor, space, scratch):
    width = factor.shape[-1]
    return pl.pallas_call(
        body,
        out_shape=shape,
        in_specs=[pl.BlockSpec(memory_space=pltpu.HBM)],
        out_specs=pl.BlockSpec(memory_space=space),
        scratch_shapes=[pltpu.VMEM((width, width), BF16)] + scratch,
        compiler_params=pltpu.CompilerParams(vmem_limit_bytes=60 * 1024 * 1024),
    )(factor)


def leaf_kernel(slices, y0, out, own_out):
    top, piece, width = slices.shape
    own = slices[...].reshape(top * piece, width).astype(BF16)
    own_out[...] = own
    out[...] = product(own, y0[...]).reshape(out.shape)


def sum_kernel(line, first, start, stop, table, got, out):
    total = table[line, first:first + 1] * got[0]
    for k in range(1, got.shape[0]):
        total = total + table[line, first + k:first + k + 1] * got[k]
    for k in range(out.shape[0]):
        out[k] = total if start <= k < stop else jnp.zeros_like(total)


def halves(out, panel, piece):
    slices = panel.reshape(panel.shape[0] // piece, piece, panel.shape[1])
    count = slices.shape[0]
    out[:count] = slices[:, :piece // 2]
    out[count:] = slices[:, piece // 2:]


def joined(update):
    cores, parts, ny = update.shape[:3]
    return jnp.concatenate(
        [
            update[core, part, y]
            for core in range(cores)
            for y in range(ny)
            for part in range(parts)
        ],
        0,
    )


def one_kernel(update, base, up, own, rest_out, out):
    rows = own.shape[0] // 2
    rest = base[...] - update[...]
    rest_out[...] = rest
    halves(out, product(own[rows:], product(up[...], rest)), 2 * out.shape[1])


def two_kernel(update, rest_in, up, own, rest_out, out):
    rows = own.shape[0] // 2
    rest = rest_in[...] - joined(update)
    rest_out[...] = rest
    out[...] = product(own[rows:], product(up[...], rest)).reshape(out.shape)


def three_kernel(update, rest, up, low, own, y_out, out):
    rows = own.shape[0] // 2
    y = product(up[...], rest[...] - update[...])
    y_out[...] = y
    out[...] = product(own[rows:], product(low[...], y)).reshape(out.shape)


def two_back_kernel(update, y, low, own, rest_out, out):
    rows = own.shape[0] // 2
    rest = y[...] - update[...]
    rest_out[...] = rest
    halves(out, product(own[:rows], product(low[...], rest)), 2 * out.shape[1])


def one_back_kernel(update, rest, low, below, x_out, out):
    x = product(low[...], rest[...] - joined(update))
    x_out[...] = x
    out[...] = product(below[...], x).reshape(out.shape)


def order_kernel(got, out):
    ny = got.shape[1]
    for y in range(ny):
        for core in range(2):
            out[2 * y + core] = got[core, y]


def last_kernel(table, update, y0, low, x, out):
    leaf = product(low[...], y0[...] - update[...])
    out[0, 0] = jnp.where(table[HIGH, 0:1] > 0.5, x[...], leaf)


def a2a(array, axes):
    array = lax.optimization_barrier(array)
    return lax.optimization_barrier(lax.all_to_all(array, axes, 0, 0, tiled=True))


def per_device(factor, rhs, upper_inverse, lower_inverse, parents, block_mask):
    ny, nz = lax.axis_size("y"), lax.axis_size("z")
    ncol = ny * lax.axis_size("core")
    base = rhs[0, 0]
    up = upper_inverse[0, 0]
    low = lower_inverse[0, 0]
    width, nrhs = base.shape
    piece = width // ncol
    count = parents.shape[0]
    top = count // 2
    late = count - nz
    row = lax.axis_index(ROW)
    col = lax.axis_index(COL)
    panel = shape_of(width, nrhs)
    half_to_top = shape_of(top, piece // 2, nrhs)
    copies = shape_of(ny, piece, nrhs)
    across = shape_of(2 * ny, piece, nrhs)
    to_top = shape_of(top, piece, nrhs)
    to_late = shape_of(nz, piece, nrhs)

    sent = slot_call(
        turn_kernel, shape_of(ncol, piece, width), factor, pltpu.HBM,
        [
            pltpu.VMEM((ncol, piece, width), F32),
            pltpu.SemaphoreType.DMA((width // 128,)),
            pltpu.SemaphoreType.DMA((ncol,)),
        ],
    )
    below = slot_call(
        turn_whole_kernel, shape_of(width, width, kind=BF16), factor, pltpu.VMEM,
        [pltpu.SemaphoreType.DMA],
    )
    table = call(
        table_kernel, shape_of(HIGH + 1, count, nrhs),
        jnp.stack([row, col]).astype(jnp.int32), parents[None, :], parents[:, None],
        block_mask, scalars=1,
    )
    y0 = jnp.dot(up.astype(F32), base, precision=lax.Precision.HIGHEST)

    slices = lax.all_to_all(sent, COL, 0, 0, tiled=True)
    table, y0, base, up, low, below, slices = lax.optimization_barrier(
        (table, y0, base, up, low, below, slices)
    )

    def total(line, first, got, shape, start=0, stop=ncol):
        body = functools.partial(sum_kernel, line, first, start, stop)
        return call(body, shape, table, got)

    def whole(half):
        return lax.all_gather(half, "core", tiled=True).reshape(width, nrhs)

    def spread(copied):
        return whole(a2a(copied, "y"))

    def spread_halves(copied):
        both = lax.all_gather(a2a(copied, BESIDE), "core", tiled=True)
        return both.reshape(ncol // ny, 2, ny, piece // 2, nrhs)

    out, own = call(leaf_kernel, (to_top, shape_of(width, width, kind=BF16)), slices, y0)
    got = total(FROM_LEAF, 0, a2a(out, HALF), across, start=ny)
    update = whole(a2a(got, ACROSS)[:ny])
    rest, out = call(one_kernel, (panel, half_to_top), update, base, up, own)
    got = total(FROM_ONE, top, a2a(out, HALF), half_to_top, start=ny)
    rest, out = call(
        two_kernel, (panel, to_late), spread_halves(got), rest, up, own
    )
    got = total(FROM_TWO, late, a2a(out, "z"), copies)
    y, out = call(three_kernel, (panel, to_late), spread(got), rest, up, low, own)
    got = total(FROM_THREE, late, a2a(out, "z"), copies)
    rest, out = call(two_back_kernel, (panel, half_to_top), spread(got), y, low, own)
    got = total(FROM_ABOVE, top, a2a(out, HALF), half_to_top, stop=ny)
    x, out = call(
        one_back_kernel, (panel, to_top), spread_halves(got), rest, low, below
    )
    got = total(TO_COLUMN, top, a2a(out, HALF), across, stop=ny)
    got = a2a(got, ACROSS)[ny:]
    got = lax.all_gather(got, "core")
    out = call(order_kernel, to_top, got)
    update = a2a(out, HALF).reshape(width, nrhs)
    return call(
        last_kernel, shape_of(1, 1, width, nrhs), table, update, y0, low, x
    )


def solution(mesh):
    grid = Mesh(mesh.devices.reshape(2, 2, 8, 8, 2), ("xh", "xl", "z", "y", "core"))
    placed = (
        P(ROW, None, COL, None, None, None),
        P(ROW, None, None, None),
        P(ROW, None, None, None),
        P(ROW, None, None, None),
        P(),
        P(),
    )
    return jax.shard_map(
        per_device,
        mesh=grid,
        in_specs=placed,
        out_specs=P(ROW, None, None, None),
        check_vma=False,
    )
```

```python
import functools

import jax
import jax.numpy as jnp
from jax import lax
from jax.experimental import pallas as pl
from jax.experimental.pallas import tpu as pltpu
from jax.sharding import Mesh, PartitionSpec as P

LEVELS = 4
HALF = ("xl", "z")
ROW = ("xh", "xl", "z")
COL = ("y", "core")
ACROSS = ("xh", "y")
BESIDE = ("xl", "y")
F32 = jnp.float32
BF16 = jnp.bfloat16
ROOMY = pltpu.CompilerParams(vmem_limit_bytes=40 * 1024 * 1024)
VM = pl.BlockSpec(memory_space=pltpu.VMEM)
SM = pl.BlockSpec(memory_space=pltpu.SMEM)

FROM_LEAF, FROM_ONE, FROM_TWO, FROM_THREE, FROM_ABOVE, TO_COLUMN, HIGH = range(7)


def shape_of(*dims, kind=F32):
    return jax.ShapeDtypeStruct(dims, kind)


def call(body, shape, *args, scalars=0):
    out = [VM] * len(shape) if isinstance(shape, tuple) else VM
    return pl.pallas_call(
        body,
        out_shape=shape,
        in_specs=[SM] * scalars + [VM] * (len(args) - scalars),
        out_specs=out,
        compiler_params=ROOMY,
    )(*args)


def product(matrix, panel):
    cols = panel.shape[1]
    high = panel.astype(BF16).astype(F32)
    rest = panel - high
    mid = rest.astype(BF16).astype(F32)
    parts = jnp.concatenate([high, mid, rest - mid], 1).astype(BF16)
    full = jnp.dot(matrix, parts, preferred_element_type=F32)
    return full[:, :cols] + full[:, cols:2 * cols] + full[:, 2 * cols:]


def table_kernel(at, parents_row, parents_col, mask, out):
    count = mask.shape[0]
    top = count // 2
    row, col = at[0], at[1]
    down = lax.broadcasted_iota(jnp.int32, (count, count), 0)
    across = lax.broadcasted_iota(jnp.int32, (count, count), 1)
    step = (parents_col[...] == across).astype(F32)
    step_t = (parents_row[...] == down).astype(F32)
    identity = (down == across).astype(F32)
    anc = power = anc_t = power_t = identity
    for _ in range(LEVELS - 1):
        power = jnp.dot(power, step, preferred_element_type=F32)
        power_t = jnp.dot(step_t, power_t, preferred_element_type=F32)
        anc = anc + power
        anc_t = anc_t + power_t
    weights = mask[...].astype(F32) * (1.0 - identity)
    upper = weights * jnp.minimum(anc, 1.0)
    lower = weights * jnp.minimum(anc_t, 1.0)

    def column(matrix, index):
        return jnp.sum(jnp.where(across == index, matrix, 0.0), axis=1, keepdims=True)

    def level(ids):
        total = jnp.zeros_like(ids)
        for depth in range(1, LEVELS):
            total = total + (ids >= count - count // 2**depth).astype(jnp.int32)
        return total

    levels = level(lax.broadcasted_iota(jnp.int32, (count, 1), 0))
    mine = level(jnp.full((count, 1), row, jnp.int32))
    low = (mine == 0).astype(F32)
    high = (mine >= 1).astype(F32)
    late = (mine >= 2).astype(F32)
    image = jnp.where(row < top, row + top, row)
    below_late = row + jnp.where(row < count - top // 2, top // 2, 0)
    above_one = row - jnp.where(row >= count - top // 2, top // 2, 0)
    lines = [
        column(upper, image) * (levels == 0).astype(F32) * low,
        column(upper, below_late) * (levels == 1).astype(F32) * high,
        column(upper, row) * (levels == 2).astype(F32) * late,
        column(lower, row) * (levels == 3).astype(F32) * late,
        column(lower, above_one) * high,
        column(lower, col) * high,
        high,
    ]
    for index, values in enumerate(lines):
        out[index] = jnp.broadcast_to(values, (count, out.shape[2]))


def turn_kernel(at, block, keep, send):
    rows = keep.shape[0]
    turned = block[0, 0, 0, 0].astype(F32).T
    mine = at[0] == 0
    keep[...] = jnp.where(mine, turned[:rows], turned[rows:])
    send[...] = jnp.where(mine, turned[rows:], turned[:rows])


def parcel_kernel(own, other, out):
    ny, piece = out.shape[0], out.shape[1] // 2
    for y in range(ny):
        out[y, :piece] = own[y * piece:(y + 1) * piece]
        out[y, piece:] = other[y * piece:(y + 1) * piece]


def turn_whole_kernel(blocks, out, block, arrived):
    copy = pltpu.make_async_copy(blocks.at[0, 0, 0, 0], block, arrived)
    copy.start()
    copy.wait()
    out[...] = block[...].astype(F32).T.astype(BF16)


def slot_call(body, shape, factor, space, scratch):
    width = factor.shape[-1]
    return pl.pallas_call(
        body,
        out_shape=shape,
        in_specs=[pl.BlockSpec(memory_space=pltpu.HBM)],
        out_specs=pl.BlockSpec(memory_space=space),
        scratch_shapes=[pltpu.VMEM((width, width), BF16)] + scratch,
        compiler_params=pltpu.CompilerParams(vmem_limit_bytes=60 * 1024 * 1024),
    )(factor)


def leaf_kernel(at, slices, y0, out, own_out):
    ny, piece = slices.shape[0], slices.shape[1] // 2
    for y in range(ny):
        first = pl.multiple_of((2 * y + at[0]) * piece, piece)
        second = pl.multiple_of((2 * y + 1 - at[0]) * piece, piece)
        own_out[pl.ds(first, piece), :] = slices[y, :piece].astype(BF16)
        own_out[pl.ds(second, piece), :] = slices[y, piece:].astype(BF16)
    out[...] = product(own_out[...], y0[...]).reshape(out.shape)


def sum_kernel(line, first, start, stop, table, got, out):
    total = table[line, first:first + 1] * got[0]
    for k in range(1, got.shape[0]):
        total = total + table[line, first + k:first + k + 1] * got[k]
    for k in range(out.shape[0]):
        out[k] = total if start <= k < stop else jnp.zeros_like(total)


def halves(out, panel, piece):
    slices = panel.reshape(panel.shape[0] // piece, piece, panel.shape[1])
    count = slices.shape[0]
    out[:count] = slices[:, :piece // 2]
    out[count:] = slices[:, piece // 2:]


def joined(update):
    cores, parts, ny = update.shape[:3]
    return jnp.concatenate(
        [
            update[core, part, y]
            for core in range(cores)
            for y in range(ny)
            for part in range(parts)
        ],
        0,
    )


def one_kernel(update, base, up, own, rest_out, out):
    rows = own.shape[0] // 2
    rest = base[...] - update[...]
    rest_out[...] = rest
    halves(out, product(own[rows:], product(up[...], rest)), 2 * out.shape[1])


def two_kernel(update, rest_in, up, own, rest_out, out):
    rows = own.shape[0] // 2
    rest = rest_in[...] - joined(update)
    rest_out[...] = rest
    out[...] = product(own[rows:], product(up[...], rest)).reshape(out.shape)


def three_kernel(update, rest, up, low, own, y_out, out):
    rows = own.shape[0] // 2
    y = product(up[...], rest[...] - update[...])
    y_out[...] = y
    out[...] = product(own[rows:], product(low[...], y)).reshape(out.shape)


def two_back_kernel(update, y, low, own, rest_out, out):
    rows = own.shape[0] // 2
    rest = y[...] - update[...]
    rest_out[...] = rest
    halves(out, product(own[:rows], product(low[...], rest)), 2 * out.shape[1])


def one_back_kernel(update, rest, low, below, x_out, out):
    x = product(low[...], rest[...] - joined(update))
    x_out[...] = x
    out[...] = product(below[...], x).reshape(out.shape)


def order_kernel(got, out):
    ny = got.shape[1]
    for y in range(ny):
        for core in range(2):
            out[2 * y + core] = got[core, y]


def last_kernel(table, update, y0, low, x, out):
    leaf = product(low[...], y0[...] - update[...])
    out[0, 0] = jnp.where(table[HIGH, 0:1] > 0.5, x[...], leaf)


def a2a(array, axes):
    array = lax.optimization_barrier(array)
    return lax.optimization_barrier(lax.all_to_all(array, axes, 0, 0, tiled=True))


def per_device(factor, rhs, upper_inverse, lower_inverse, parents, block_mask):
    ny, nz = lax.axis_size("y"), lax.axis_size("z")
    ncol = ny * lax.axis_size("core")
    base = rhs[0, 0]
    up = upper_inverse[0, 0]
    low = lower_inverse[0, 0]
    width, nrhs = base.shape
    piece = width // ncol
    count = parents.shape[0]
    top = count // 2
    late = count - nz
    row = lax.axis_index(ROW)
    col = lax.axis_index(COL)
    panel = shape_of(width, nrhs)
    half_to_top = shape_of(top, piece // 2, nrhs)
    copies = shape_of(ny, piece, nrhs)
    across = shape_of(2 * ny, piece, nrhs)
    to_top = shape_of(top, piece, nrhs)
    to_late = shape_of(nz, piece, nrhs)

    core = lax.axis_index("core")[None].astype(jnp.int32)
    half_block = shape_of(width // 2, width)
    keep, send = pl.pallas_call(
        turn_kernel,
        out_shape=(half_block, half_block),
        grid=(1,),
        in_specs=[
            SM,
            pl.BlockSpec((1, 1, 1, 1, width, width), lambda k: (0, 0, 0, 1, 0, 0)),
        ],
        out_specs=(
            pl.BlockSpec((width // 2, width), lambda k: (0, 0)),
            pl.BlockSpec((width // 2, width), lambda k: (0, 0)),
        ),
        compiler_params=ROOMY,
    )(core, factor)
    other = lax.ppermute(send, "core", [(0, 1), (1, 0)])
    below = slot_call(
        turn_whole_kernel, shape_of(width, width, kind=BF16), factor, pltpu.VMEM,
        [pltpu.SemaphoreType.DMA],
    )
    table = call(
        table_kernel, shape_of(HIGH + 1, count, nrhs),
        jnp.stack([row, col]).astype(jnp.int32), parents[None, :], parents[:, None],
        block_mask, scalars=1,
    )
    y0 = jnp.dot(up.astype(F32), base, precision=lax.Precision.HIGHEST)

    parcels = call(parcel_kernel, shape_of(ny, 2 * piece, width), keep, other)
    table, y0, base, up, low, below, parcels = lax.optimization_barrier(
        (table, y0, base, up, low, below, parcels)
    )
    slices = a2a(parcels, "y")

    def total(line, first, got, shape, start=0, stop=ncol):
        body = functools.partial(sum_kernel, line, first, start, stop)
        return call(body, shape, table, got)

    def whole(half):
        return lax.all_gather(half, "core", tiled=True).reshape(width, nrhs)

    def spread(copied):
        return whole(a2a(copied, "y"))

    def spread_halves(copied):
        both = lax.all_gather(a2a(copied, BESIDE), "core", tiled=True)
        return both.reshape(ncol // ny, 2, ny, piece // 2, nrhs)

    out, own = call(leaf_kernel, (to_top, shape_of(width, width, kind=BF16)), core, slices, y0, scalars=1)
    got = total(FROM_LEAF, 0, a2a(out, HALF), across, start=ny)
    update = whole(a2a(got, ACROSS)[:ny])
    rest, out = call(one_kernel, (panel, half_to_top), update, base, up, own)
    got = total(FROM_ONE, top, a2a(out, HALF), half_to_top, start=ny)
    rest, out = call(
        two_kernel, (panel, to_late), spread_halves(got), rest, up, own
    )
    got = total(FROM_TWO, late, a2a(out, "z"), copies)
    y, out = call(three_kernel, (panel, to_late), spread(got), rest, up, low, own)
    got = total(FROM_THREE, late, a2a(out, "z"), copies)
    rest, out = call(two_back_kernel, (panel, half_to_top), spread(got), y, low, own)
    got = total(FROM_ABOVE, top, a2a(out, HALF), half_to_top, stop=ny)
    x, out = call(
        one_back_kernel, (panel, to_top), spread_halves(got), rest, low, below
    )
    got = total(TO_COLUMN, top, a2a(out, HALF), across, stop=ny)
    got = a2a(got, ACROSS)[ny:]
    got = lax.all_gather(got, "core")
    out = call(order_kernel, to_top, got)
    update = a2a(out, HALF).reshape(width, nrhs)
    return call(
        last_kernel, shape_of(1, 1, width, nrhs), table, update, y0, low, x
    )


def solution(mesh):
    grid = Mesh(mesh.devices.reshape(2, 2, 8, 8, 2), ("xh", "xl", "z", "y", "core"))
    placed = (
        P(ROW, None, COL, None, None, None),
        P(ROW, None, None, None),
        P(ROW, None, None, None),
        P(ROW, None, None, None),
        P(),
        P(),
    )
    return jax.shard_map(
        per_device,
        mesh=grid,
        in_specs=placed,
        out_specs=P(ROW, None, None, None),
        check_vma=False,
    )
```

```python
import functools

import jax
import jax.numpy as jnp
from jax import lax
from jax.experimental import pallas as pl
from jax.experimental.pallas import tpu as pltpu
from jax.sharding import Mesh, PartitionSpec as P

LEVELS = 4
HALF = ("z", "xl")
ROW = ("xh", "xl", "z")
COL = ("y", "core")
SLICES = ("core", "y")
ACROSS = ("y", "xh")
BESIDE = ("y", "xl")
F32 = jnp.float32
BF16 = jnp.bfloat16
ROOMY = pltpu.CompilerParams(vmem_limit_bytes=40 * 1024 * 1024)
VM = pl.BlockSpec(memory_space=pltpu.VMEM)
SM = pl.BlockSpec(memory_space=pltpu.SMEM)

FROM_LEAF, FROM_ONE, FROM_TWO, FROM_THREE, FROM_ABOVE, TO_COLUMN, HIGH = range(7)


def shape_of(*dims, kind=F32):
    return jax.ShapeDtypeStruct(dims, kind)


def call(body, shape, *args, scalars=0):
    out = [VM] * len(shape) if isinstance(shape, tuple) else VM
    return pl.pallas_call(
        body,
        out_shape=shape,
        in_specs=[SM] * scalars + [VM] * (len(args) - scalars),
        out_specs=out,
        compiler_params=ROOMY,
    )(*args)


def product(matrix, panel):
    cols = panel.shape[1]
    high = panel.astype(BF16).astype(F32)
    rest = panel - high
    mid = rest.astype(BF16).astype(F32)
    parts = jnp.concatenate([high, mid, rest - mid], 1).astype(BF16)
    full = jnp.dot(matrix, parts, preferred_element_type=F32)
    return full[:, :cols] + full[:, cols:2 * cols] + full[:, 2 * cols:]


def table_kernel(at, parents_row, parents_col, mask, out):
    count = mask.shape[0]
    top = count // 2
    row, col = at[0], at[1]
    down = lax.broadcasted_iota(jnp.int32, (count, count), 0)
    across = lax.broadcasted_iota(jnp.int32, (count, count), 1)
    step = (parents_col[...] == across).astype(F32)
    step_t = (parents_row[...] == down).astype(F32)
    identity = (down == across).astype(F32)
    anc = power = anc_t = power_t = identity
    for _ in range(LEVELS - 1):
        power = jnp.dot(power, step, preferred_element_type=F32)
        power_t = jnp.dot(step_t, power_t, preferred_element_type=F32)
        anc = anc + power
        anc_t = anc_t + power_t
    weights = mask[...].astype(F32) * (1.0 - identity)
    upper = weights * jnp.minimum(anc, 1.0)
    lower = weights * jnp.minimum(anc_t, 1.0)

    def column(matrix, index):
        return jnp.sum(jnp.where(across == index, matrix, 0.0), axis=1, keepdims=True)

    def level(ids):
        total = jnp.zeros_like(ids)
        for depth in range(1, LEVELS):
            total = total + (ids >= count - count // 2**depth).astype(jnp.int32)
        return total

    levels = level(lax.broadcasted_iota(jnp.int32, (count, 1), 0))
    mine = level(jnp.full((count, 1), row, jnp.int32))
    low = (mine == 0).astype(F32)
    high = (mine >= 1).astype(F32)
    late = (mine >= 2).astype(F32)
    image = jnp.where(row < top, row + top, row)
    below_late = row + jnp.where(row < count - top // 2, top // 2, 0)
    above_one = row - jnp.where(row >= count - top // 2, top // 2, 0)
    lines = [
        column(upper, image) * (levels == 0).astype(F32) * low,
        column(upper, below_late) * (levels == 1).astype(F32) * high,
        column(upper, row) * (levels == 2).astype(F32) * late,
        column(lower, row) * (levels == 3).astype(F32) * late,
        column(lower, above_one) * high,
        column(lower, col) * high,
        high,
    ]
    for index, values in enumerate(lines):
        out[index] = jnp.broadcast_to(values, (count, out.shape[2]))


def turn_kernel(blocks, out, block, turned, arrived, gone):
    piece = turned.shape[1]
    part = 128
    inward = []
    for k in range(block.shape[1] // part):
        lanes = pl.ds(k * part, part)
        copy = pltpu.make_async_copy(
            blocks.at[0, 0, 0, 1, :, lanes], block.at[:, lanes], arrived.at[k]
        )
        copy.start()
        inward.append(copy)
    outward = []
    for k, copy in enumerate(inward):
        copy.wait()
        rows = block[:, k * part:(k + 1) * part].astype(F32).T
        for j in range(part // piece):
            to = k * (part // piece) + j
            turned[to] = rows[j * piece:(j + 1) * piece]
            copy = pltpu.make_async_copy(turned.at[to], out.at[to], gone.at[to])
            copy.start()
            outward.append(copy)
    for copy in outward:
        copy.wait()


def turn_whole_kernel(blocks, out, block, arrived):
    copy = pltpu.make_async_copy(blocks.at[0, 0, 0, 0], block, arrived)
    copy.start()
    copy.wait()
    out[...] = block[...].astype(F32).T.astype(BF16)


def slot_call(body, shape, factor, space, scratch):
    width = factor.shape[-1]
    return pl.pallas_call(
        body,
        out_shape=shape,
        in_specs=[pl.BlockSpec(memory_space=pltpu.HBM)],
        out_specs=pl.BlockSpec(memory_space=space),
        scratch_shapes=[pltpu.VMEM((width, width), BF16)] + scratch,
        compiler_params=pltpu.CompilerParams(vmem_limit_bytes=60 * 1024 * 1024),
    )(factor)


def paired(k, count):
    return 2 * (k % (count // 2)) + k // (count // 2)


def leaf_kernel(slices, y0, out, own_out):
    top, piece, width = slices.shape
    ny = top // 2
    own = jnp.concatenate(
        [slices[core * ny + y] for y in range(ny) for core in range(2)], 0
    ).astype(BF16)
    own_out[...] = own
    result = product(own, y0[...])
    for k in range(top):
        out[paired(k, top)] = result[k * piece:(k + 1) * piece]


def sum_kernel(line, first, pairs, side, table, got, out):
    count = got.shape[0]
    total = jnp.zeros(got.shape[1:], F32)
    for k in range(count):
        at = paired(k, count) if pairs else k
        total = total + table[line, first + k:first + k + 1] * got[at]
    for k in range(out.shape[0]):
        out[k] = total if side is None or k % 2 == side else jnp.zeros_like(total)


def one_kernel(update, base, up, own, rest_out, out):
    rows = own.shape[0] // 2
    rest = base[...] - update[...]
    rest_out[...] = rest
    out[...] = product(own[rows:], product(up[...], rest)).reshape(out.shape)


def two_kernel(update, rest_in, up, own, rest_out, out):
    rows = own.shape[0] // 2
    rest = rest_in[...] - update[...]
    rest_out[...] = rest
    out[...] = product(own[rows:], product(up[...], rest)).reshape(out.shape)


def three_kernel(update, rest, up, low, own, y_out, out):
    rows = own.shape[0] // 2
    y = product(up[...], rest[...] - update[...])
    y_out[...] = y
    out[...] = product(own[rows:], product(low[...], y)).reshape(out.shape)


def two_back_kernel(update, y, low, own, rest_out, out):
    rows = own.shape[0] // 2
    rest = y[...] - update[...]
    rest_out[...] = rest
    out[...] = product(own[:rows], product(low[...], rest)).reshape(out.shape)


def one_back_kernel(update, rest, low, below, x_out, out):
    x = product(low[...], rest[...] - update[...])
    x_out[...] = x
    out[...] = product(below[...], x).reshape(out.shape)


def order_kernel(got, out):
    ny = got.shape[1]
    for y in range(ny):
        for core in range(2):
            out[paired(2 * y + core, 2 * ny)] = got[core, y]


def last_kernel(table, update, y0, low, x, out):
    leaf = product(low[...], y0[...] - update[...])
    out[0, 0] = jnp.where(table[HIGH, 0:1] > 0.5, x[...], leaf)


def a2a(array, axes):
    array = lax.optimization_barrier(array)
    return lax.optimization_barrier(lax.all_to_all(array, axes, 0, 0, tiled=True))


def per_device(factor, rhs, upper_inverse, lower_inverse, parents, block_mask):
    ny, nz = lax.axis_size("y"), lax.axis_size("z")
    ncol = ny * lax.axis_size("core")
    base = rhs[0, 0]
    up = upper_inverse[0, 0]
    low = lower_inverse[0, 0]
    width, nrhs = base.shape
    piece = width // ncol
    count = parents.shape[0]
    top = count // 2
    late = count - nz
    row = lax.axis_index(ROW)
    col = lax.axis_index(COL)
    panel = shape_of(width, nrhs)
    half_to_top = shape_of(top, piece // 2, nrhs)
    copies = shape_of(ny, piece, nrhs)
    across = shape_of(2 * ny, piece, nrhs)
    to_top = shape_of(top, piece, nrhs)
    to_late = shape_of(nz, piece, nrhs)

    sent = slot_call(
        turn_kernel, shape_of(ncol, piece, width), factor, pltpu.HBM,
        [
            pltpu.VMEM((ncol, piece, width), F32),
            pltpu.SemaphoreType.DMA((width // 128,)),
            pltpu.SemaphoreType.DMA((ncol,)),
        ],
    )
    below = slot_call(
        turn_whole_kernel, shape_of(width, width, kind=BF16), factor, pltpu.VMEM,
        [pltpu.SemaphoreType.DMA],
    )
    table = call(
        table_kernel, shape_of(HIGH + 1, count, nrhs),
        jnp.stack([row, col]).astype(jnp.int32), parents[None, :], parents[:, None],
        block_mask, scalars=1,
    )
    y0 = jnp.dot(up.astype(F32), base, precision=lax.Precision.HIGHEST)

    slices = lax.all_to_all(sent, SLICES, 0, 0, tiled=True)
    table, y0, base, up, low, below, slices = lax.optimization_barrier(
        (table, y0, base, up, low, below, slices)
    )

    def total(line, first, got, shape, pairs=True, side=None):
        body = functools.partial(sum_kernel, line, first, pairs, side)
        return call(body, shape, table, got)

    def whole(part):
        return lax.all_gather(part, "core", tiled=True).reshape(width, nrhs)

    def spread(copied, axes):
        return whole(a2a(copied, axes))

    def from_side(copied, side):
        return a2a(copied, ACROSS).reshape(ny, 2, piece, nrhs)[:, side]

    out, own = call(leaf_kernel, (to_top, shape_of(width, width, kind=BF16)), slices, y0)
    got = total(FROM_LEAF, 0, a2a(out, HALF), across, side=1)
    update = whole(from_side(got, 0))
    rest, out = call(one_kernel, (panel, half_to_top), update, base, up, own)
    got = total(FROM_ONE, top, a2a(out, HALF), half_to_top, side=1)
    rest, out = call(
        two_kernel, (panel, to_late), spread(got, BESIDE), rest, up, own
    )
    got = total(FROM_TWO, late, a2a(out, "z"), copies, pairs=False)
    y, out = call(three_kernel, (panel, to_late), spread(got, "y"), rest, up, low, own)
    got = total(FROM_THREE, late, a2a(out, "z"), copies, pairs=False)
    rest, out = call(two_back_kernel, (panel, half_to_top), spread(got, "y"), y, low, own)
    got = total(FROM_ABOVE, top, a2a(out, HALF), half_to_top, side=0)
    x, out = call(
        one_back_kernel, (panel, to_top), spread(got, BESIDE), rest, low, below
    )
    got = total(TO_COLUMN, top, a2a(out, HALF), across, side=0)
    got = lax.all_gather(from_side(got, 1), "core")
    out = call(order_kernel, to_top, got)
    update = a2a(out, HALF).reshape(width, nrhs)
    return call(
        last_kernel, shape_of(1, 1, width, nrhs), table, update, y0, low, x
    )


def solution(mesh):
    grid = Mesh(mesh.devices.reshape(2, 2, 8, 8, 2), ("xh", "xl", "z", "y", "core"))
    placed = (
        P(ROW, None, COL, None, None, None),
        P(ROW, None, None, None),
        P(ROW, None, None, None),
        P(ROW, None, None, None),
        P(),
        P(),
    )
    return jax.shard_map(
        per_device,
        mesh=grid,
        in_specs=placed,
        out_specs=P(ROW, None, None, None),
        check_vma=False,
    )
```

```python
import functools

import jax
import jax.numpy as jnp
from jax import lax
from jax.experimental import pallas as pl
from jax.experimental.pallas import tpu as pltpu
from jax.sharding import Mesh, PartitionSpec as P

LEVELS = 4
HALF = ("xl", "z")
ROW = ("xh", "xl", "z")
COL = ("y", "core")
ACROSS = ("xh", "y")
BESIDE = ("y", "xl")
F32 = jnp.float32
BF16 = jnp.bfloat16
ROOMY = pltpu.CompilerParams(vmem_limit_bytes=40 * 1024 * 1024)
VM = pl.BlockSpec(memory_space=pltpu.VMEM)
SM = pl.BlockSpec(memory_space=pltpu.SMEM)

FROM_LEAF, FROM_ONE, FROM_TWO, FROM_THREE, FROM_ABOVE, TO_COLUMN, HIGH = range(7)


def shape_of(*dims, kind=F32):
    return jax.ShapeDtypeStruct(dims, kind)


def call(body, shape, *args, scalars=0):
    out = [VM] * len(shape) if isinstance(shape, tuple) else VM
    return pl.pallas_call(
        body,
        out_shape=shape,
        in_specs=[SM] * scalars + [VM] * (len(args) - scalars),
        out_specs=out,
        compiler_params=ROOMY,
    )(*args)


def product(matrix, panel):
    cols = panel.shape[1]
    high = panel.astype(BF16).astype(F32)
    rest = panel - high
    mid = rest.astype(BF16).astype(F32)
    parts = jnp.concatenate([high, mid, rest - mid], 1).astype(BF16)
    full = jnp.dot(matrix, parts, preferred_element_type=F32)
    return full[:, :cols] + full[:, cols:2 * cols] + full[:, 2 * cols:]


def table_kernel(at, parents_row, parents_col, mask, out):
    count = mask.shape[0]
    top = count // 2
    row, col = at[0], at[1]
    down = lax.broadcasted_iota(jnp.int32, (count, count), 0)
    across = lax.broadcasted_iota(jnp.int32, (count, count), 1)
    step = (parents_col[...] == across).astype(F32)
    step_t = (parents_row[...] == down).astype(F32)
    identity = (down == across).astype(F32)
    anc = power = anc_t = power_t = identity
    for _ in range(LEVELS - 1):
        power = jnp.dot(power, step, preferred_element_type=F32)
        power_t = jnp.dot(step_t, power_t, preferred_element_type=F32)
        anc = anc + power
        anc_t = anc_t + power_t
    weights = mask[...].astype(F32) * (1.0 - identity)
    upper = weights * jnp.minimum(anc, 1.0)
    lower = weights * jnp.minimum(anc_t, 1.0)

    def column(matrix, index):
        return jnp.sum(jnp.where(across == index, matrix, 0.0), axis=1, keepdims=True)

    def level(ids):
        total = jnp.zeros_like(ids)
        for depth in range(1, LEVELS):
            total = total + (ids >= count - count // 2**depth).astype(jnp.int32)
        return total

    levels = level(lax.broadcasted_iota(jnp.int32, (count, 1), 0))
    mine = level(jnp.full((count, 1), row, jnp.int32))
    low = (mine == 0).astype(F32)
    high = (mine >= 1).astype(F32)
    late = (mine >= 2).astype(F32)
    image = jnp.where(row < top, row + top, row)
    below_late = row + jnp.where(row < count - top // 2, top // 2, 0)
    above_one = row - jnp.where(row >= count - top // 2, top // 2, 0)
    lines = [
        column(upper, image) * (levels == 0).astype(F32) * low,
        column(upper, below_late) * (levels == 1).astype(F32) * high,
        column(upper, row) * (levels == 2).astype(F32) * late,
        column(lower, row) * (levels == 3).astype(F32) * late,
        column(lower, above_one) * high,
        column(lower, col) * high,
        high,
    ]
    for index, values in enumerate(lines):
        out[index] = jnp.broadcast_to(values, (count, out.shape[2]))


def turn_kernel(blocks, out, block, turned, arrived, gone):
    ncol, piece = turned.shape[0], turned.shape[1]
    ny = ncol // 2
    part = 128
    inward = []
    for k in range(block.shape[1] // part):
        lanes = pl.ds(k * part, part)
        copy = pltpu.make_async_copy(
            blocks.at[0, 0, 0, 1, :, lanes], block.at[:, lanes], arrived.at[k]
        )
        copy.start()
        inward.append(copy)
    outward = []
    for k, copy in enumerate(inward):
        copy.wait()
        rows = block[:, k * part:(k + 1) * part].astype(F32).T
        for j in range(part // piece):
            core, y = divmod(k * (part // piece) + j, ny)
            to = 2 * y + core
            turned[to] = rows[j * piece:(j + 1) * piece]
            copy = pltpu.make_async_copy(turned.at[to], out.at[to], gone.at[to])
            copy.start()
            outward.append(copy)
    for copy in outward:
        copy.wait()


def turn_whole_kernel(blocks, out, block, arrived):
    copy = pltpu.make_async_copy(blocks.at[0, 0, 0, 0], block, arrived)
    copy.start()
    copy.wait()
    out[...] = block[...].astype(F32).T.astype(BF16)


def slot_call(body, shape, factor, space, scratch):
    width = factor.shape[-1]
    return pl.pallas_call(
        body,
        out_shape=shape,
        in_specs=[pl.BlockSpec(memory_space=pltpu.HBM)],
        out_specs=pl.BlockSpec(memory_space=space),
        scratch_shapes=[pltpu.VMEM((width, width), BF16)] + scratch,
        compiler_params=pltpu.CompilerParams(vmem_limit_bytes=60 * 1024 * 1024),
    )(factor)


def leaf_kernel(slices, y0, out, own_out):
    top, piece, width = slices.shape
    own = slices[...].reshape(top * piece, width).astype(BF16)
    own_out[...] = own
    out[...] = product(own, y0[...]).reshape(out.shape)


def sum_kernel(line, first, to, table, got, out):
    total = table[line, first:first + 1] * got[0]
    for k in range(1, got.shape[0]):
        total = total + table[line, first + k:first + k + 1] * got[k]
    for k in range(out.shape[0]):
        out[k] = total if k in to else jnp.zeros_like(total)


def halves(out, panel, piece):
    slices = panel.reshape(panel.shape[0] // piece, piece, panel.shape[1])
    count = slices.shape[0]
    out[:count] = slices[:, :piece // 2]
    out[count:] = slices[:, piece // 2:]


def one_kernel(update, base, up, own, rest_out, out):
    rows = own.shape[0] // 2
    rest = base[...] - update[...]
    rest_out[...] = rest
    halves(out, product(own[rows:], product(up[...], rest)), 2 * out.shape[1])


def two_kernel(update, rest_in, up, own, rest_out, out):
    rows = own.shape[0] // 2
    rest = rest_in[...] - update[...]
    rest_out[...] = rest
    out[...] = product(own[rows:], product(up[...], rest)).reshape(out.shape)


def three_kernel(update, rest, up, low, own, y_out, out):
    rows = own.shape[0] // 2
    y = product(up[...], rest[...] - update[...])
    y_out[...] = y
    out[...] = product(own[rows:], product(low[...], y)).reshape(out.shape)


def two_back_kernel(update, y, low, own, rest_out, out):
    rows = own.shape[0] // 2
    rest = y[...] - update[...]
    rest_out[...] = rest
    halves(out, product(own[:rows], product(low[...], rest)), 2 * out.shape[1])


def one_back_kernel(update, rest, low, below, x_out, out):
    x = product(low[...], rest[...] - update[...])
    x_out[...] = x
    out[...] = product(below[...], x).reshape(out.shape)


def order_kernel(got, out):
    ny = got.shape[1]
    for y in range(ny):
        for core in range(2):
            out[2 * y + core] = got[core, y]


def last_kernel(table, update, y0, low, x, out):
    leaf = product(low[...], y0[...] - update[...])
    out[0, 0] = jnp.where(table[HIGH, 0:1] > 0.5, x[...], leaf)


def a2a(array, axes):
    array = lax.optimization_barrier(array)
    return lax.optimization_barrier(lax.all_to_all(array, axes, 0, 0, tiled=True))


def per_device(factor, rhs, upper_inverse, lower_inverse, parents, block_mask):
    ny, nz = lax.axis_size("y"), lax.axis_size("z")
    ncol = ny * lax.axis_size("core")
    base = rhs[0, 0]
    up = upper_inverse[0, 0]
    low = lower_inverse[0, 0]
    width, nrhs = base.shape
    piece = width // ncol
    count = parents.shape[0]
    top = count // 2
    late = count - nz
    row = lax.axis_index(ROW)
    col = lax.axis_index(COL)
    panel = shape_of(width, nrhs)
    half_to_top = shape_of(top, piece // 2, nrhs)
    copies = shape_of(ny, piece, nrhs)
    across = shape_of(2 * ny, piece, nrhs)
    to_top = shape_of(top, piece, nrhs)
    to_late = shape_of(nz, piece, nrhs)

    sent = slot_call(
        turn_kernel, shape_of(ncol, piece, width), factor, pltpu.HBM,
        [
            pltpu.VMEM((ncol, piece, width), F32),
            pltpu.SemaphoreType.DMA((width // 128,)),
            pltpu.SemaphoreType.DMA((ncol,)),
        ],
    )
    below = slot_call(
        turn_whole_kernel, shape_of(width, width, kind=BF16), factor, pltpu.VMEM,
        [pltpu.SemaphoreType.DMA],
    )
    table = call(
        table_kernel, shape_of(HIGH + 1, count, nrhs),
        jnp.stack([row, col]).astype(jnp.int32), parents[None, :], parents[:, None],
        block_mask, scalars=1,
    )
    y0 = jnp.dot(up.astype(F32), base, precision=lax.Precision.HIGHEST)

    slices = lax.all_to_all(sent, COL, 0, 0, tiled=True)
    table, y0, base, up, low, below, slices = lax.optimization_barrier(
        (table, y0, base, up, low, below, slices)
    )

    def total(line, first, got, shape, to):
        body = functools.partial(sum_kernel, line, first, to)
        return call(body, shape, table, got)

    def whole(half):
        return lax.all_gather(half, "core", tiled=True).reshape(width, nrhs)

    def spread(copied):
        return whole(a2a(copied, "y"))

    def spread_halves(copied):
        return whole(a2a(copied, BESIDE))

    out, own = call(leaf_kernel, (to_top, shape_of(width, width, kind=BF16)), slices, y0)
    got = total(FROM_LEAF, 0, a2a(out, HALF), across, range(ny, ncol))
    update = whole(a2a(got, ACROSS)[:ny])
    rest, out = call(one_kernel, (panel, half_to_top), update, base, up, own)
    got = total(FROM_ONE, top, a2a(out, HALF), half_to_top, range(1, ncol, 2))
    rest, out = call(
        two_kernel, (panel, to_late), spread_halves(got), rest, up, own
    )
    got = total(FROM_TWO, late, a2a(out, "z"), copies, range(ny))
    y, out = call(three_kernel, (panel, to_late), spread(got), rest, up, low, own)
    got = total(FROM_THREE, late, a2a(out, "z"), copies, range(ny))
    rest, out = call(two_back_kernel, (panel, half_to_top), spread(got), y, low, own)
    got = total(FROM_ABOVE, top, a2a(out, HALF), half_to_top, range(0, ncol, 2))
    x, out = call(
        one_back_kernel, (panel, to_top), spread_halves(got), rest, low, below
    )
    got = total(TO_COLUMN, top, a2a(out, HALF), across, range(ny))
    got = a2a(got, ACROSS)[ny:]
    got = lax.all_gather(got, "core")
    out = call(order_kernel, to_top, got)
    update = a2a(out, HALF).reshape(width, nrhs)
    return call(
        last_kernel, shape_of(1, 1, width, nrhs), table, update, y0, low, x
    )


def solution(mesh):
    grid = Mesh(mesh.devices.reshape(2, 2, 8, 8, 2), ("xh", "xl", "z", "y", "core"))
    placed = (
        P(ROW, None, COL, None, None, None),
        P(ROW, None, None, None),
        P(ROW, None, None, None),
        P(ROW, None, None, None),
        P(),
        P(),
    )
    return jax.shard_map(
        per_device,
        mesh=grid,
        in_specs=placed,
        out_specs=P(ROW, None, None, None),
        check_vma=False,
    )
```

```python
import functools

import jax
import jax.numpy as jnp
from jax import lax
from jax.experimental import pallas as pl
from jax.experimental.pallas import tpu as pltpu
from jax.sharding import Mesh, PartitionSpec as P

LEVELS = 4
HALF = ("xl", "z")
ROW = ("xh", "xl", "z")
COL = ("y", "core")
ACROSS = ("xh", "y")
BESIDE = ("xl", "y")
F32 = jnp.float32
BF16 = jnp.bfloat16
ROOMY = pltpu.CompilerParams(vmem_limit_bytes=40 * 1024 * 1024)
VM = pl.BlockSpec(memory_space=pltpu.VMEM)
SM = pl.BlockSpec(memory_space=pltpu.SMEM)

FROM_LEAF, FROM_ONE, FROM_TWO, FROM_THREE, FROM_ABOVE, TO_COLUMN, HIGH = range(7)


def shape_of(*dims, kind=F32):
    return jax.ShapeDtypeStruct(dims, kind)


def call(body, shape, *args, scalars=0):
    out = [VM] * len(shape) if isinstance(shape, tuple) else VM
    return pl.pallas_call(
        body,
        out_shape=shape,
        in_specs=[SM] * scalars + [VM] * (len(args) - scalars),
        out_specs=out,
        compiler_params=ROOMY,
    )(*args)


def product(matrix, panel):
    cols = panel.shape[1]
    high = panel.astype(BF16).astype(F32)
    rest = panel - high
    mid = rest.astype(BF16).astype(F32)
    parts = jnp.concatenate([high, mid, rest - mid], 1).astype(BF16)
    full = jnp.dot(matrix, parts, preferred_element_type=F32)
    return full[:, :cols] + full[:, cols:2 * cols] + full[:, 2 * cols:]


def table_kernel(at, parents_row, parents_col, mask, out):
    count = mask.shape[0]
    top = count // 2
    row, col = at[0], at[1]
    down = lax.broadcasted_iota(jnp.int32, (count, count), 0)
    across = lax.broadcasted_iota(jnp.int32, (count, count), 1)
    step = (parents_col[...] == across).astype(F32)
    step_t = (parents_row[...] == down).astype(F32)
    identity = (down == across).astype(F32)
    anc = power = anc_t = power_t = identity
    for _ in range(LEVELS - 1):
        power = jnp.dot(power, step, preferred_element_type=F32)
        power_t = jnp.dot(step_t, power_t, preferred_element_type=F32)
        anc = anc + power
        anc_t = anc_t + power_t
    weights = mask[...].astype(F32) * (1.0 - identity)
    upper = weights * jnp.minimum(anc, 1.0)
    lower = weights * jnp.minimum(anc_t, 1.0)

    def column(matrix, index):
        return jnp.sum(jnp.where(across == index, matrix, 0.0), axis=1, keepdims=True)

    def level(ids):
        total = jnp.zeros_like(ids)
        for depth in range(1, LEVELS):
            total = total + (ids >= count - count // 2**depth).astype(jnp.int32)
        return total

    levels = level(lax.broadcasted_iota(jnp.int32, (count, 1), 0))
    mine = level(jnp.full((count, 1), row, jnp.int32))
    low = (mine == 0).astype(F32)
    high = (mine >= 1).astype(F32)
    late = (mine >= 2).astype(F32)
    image = jnp.where(row < top, row + top, row)
    below_late = row + jnp.where(row < count - top // 2, top // 2, 0)
    above_one = row - jnp.where(row >= count - top // 2, top // 2, 0)
    lines = [
        column(upper, image) * (levels == 0).astype(F32) * low,
        column(upper, below_late) * (levels == 1).astype(F32) * high,
        column(upper, row) * (levels == 2).astype(F32) * late,
        column(lower, row) * (levels == 3).astype(F32) * late,
        column(lower, above_one) * high,
        column(lower, col) * high,
        high,
    ]
    for index, values in enumerate(lines):
        out[index] = jnp.broadcast_to(values, (count, out.shape[2]))


def turn_kernel(blocks, out, block, turned, arrived, gone):
    ncol, piece = turned.shape[0], turned.shape[1]
    ny = ncol // 2
    part = 128
    inward = []
    for k in range(block.shape[1] // part):
        lanes = pl.ds(k * part, part)
        copy = pltpu.make_async_copy(
            blocks.at[0, 0, 0, 1, :, lanes], block.at[:, lanes], arrived.at[k]
        )
        copy.start()
        inward.append(copy)
    outward = []
    for k, copy in enumerate(inward):
        copy.wait()
        rows = block[:, k * part:(k + 1) * part].astype(F32).T
        for j in range(part // piece):
            core, y = divmod(k * (part // piece) + j, ny)
            to = 2 * y + core
            turned[to] = rows[j * piece:(j + 1) * piece]
            copy = pltpu.make_async_copy(turned.at[to], out.at[to], gone.at[to])
            copy.start()
            outward.append(copy)
    for copy in outward:
        copy.wait()


def turn_whole_kernel(blocks, out, block, arrived):
    copy = pltpu.make_async_copy(blocks.at[0, 0, 0, 0], block, arrived)
    copy.start()
    copy.wait()
    out[...] = block[...].astype(F32).T.astype(BF16)


def slot_call(body, shape, factor, space, scratch):
    width = factor.shape[-1]
    return pl.pallas_call(
        body,
        out_shape=shape,
        in_specs=[pl.BlockSpec(memory_space=pltpu.HBM)],
        out_specs=pl.BlockSpec(memory_space=space),
        scratch_shapes=[pltpu.VMEM((width, width), BF16)] + scratch,
        compiler_params=pltpu.CompilerParams(vmem_limit_bytes=60 * 1024 * 1024),
    )(factor)


def leaf_kernel(slices, y0, out, own_out):
    top, piece, width = slices.shape
    own = slices[...].reshape(top * piece, width).astype(BF16)
    own_out[...] = own
    out[...] = product(own, y0[...]).reshape(out.shape)


def sum_kernel(line, first, start, stop, table, got, out):
    total = table[line, first:first + 1] * got[0]
    for k in range(1, got.shape[0]):
        total = total + table[line, first + k:first + k + 1] * got[k]
    for k in range(out.shape[0]):
        out[k] = total if start <= k < stop else jnp.zeros_like(total)


def halves(out, panel, piece):
    slices = panel.reshape(panel.shape[0] // piece, piece, panel.shape[1])
    count = slices.shape[0]
    out[:count] = slices[:, :piece // 2]
    out[count:] = slices[:, piece // 2:]


def joined(update):
    cores, parts, ny = update.shape[:3]
    return jnp.concatenate(
        [
            update[core, part, y]
            for core in range(cores)
            for y in range(ny)
            for part in range(parts)
        ],
        0,
    )


def one_kernel(update, base, up, own, rest_out, out):
    rows = own.shape[0] // 2
    rest = base[...] - update[...]
    rest_out[...] = rest
    halves(out, product(own[rows:], product(up[...], rest)), 2 * out.shape[1])


def two_kernel(update, rest_in, up, own, rest_out, out):
    rows = own.shape[0] // 2
    rest = rest_in[...] - joined(update)
    rest_out[...] = rest
    out[...] = product(own[rows:], product(up[...], rest)).reshape(out.shape)


def three_kernel(update, rest, up, low, own, y_out, out):
    rows = own.shape[0] // 2
    y = product(up[...], rest[...] - update[...])
    y_out[...] = y
    out[...] = product(own[rows:], product(low[...], y)).reshape(out.shape)


def two_back_kernel(update, y, low, own, rest_out, out):
    rows = own.shape[0] // 2
    rest = y[...] - update[...]
    rest_out[...] = rest
    halves(out, product(own[:rows], product(low[...], rest)), 2 * out.shape[1])


def one_back_kernel(update, rest, low, below, x_out, out):
    x = product(low[...], rest[...] - joined(update))
    x_out[...] = x
    out[...] = product(below[...], x).reshape(out.shape)


def order_kernel(got, out):
    ny = got.shape[1]
    for y in range(ny):
        for core in range(2):
            out[2 * y + core] = got[core, y]


def last_kernel(table, update, y0, low, x, out):
    leaf = product(low[...], y0[...] - update[...])
    out[0, 0] = jnp.where(table[HIGH, 0:1] > 0.5, x[...], leaf)


def a2a(array, axes):
    array = lax.optimization_barrier(array)
    return lax.optimization_barrier(lax.all_to_all(array, axes, 0, 0, tiled=True))


def per_device(factor, rhs, upper_inverse, lower_inverse, parents, block_mask):
    ny, nz = lax.axis_size("y"), lax.axis_size("z")
    ncol = ny * lax.axis_size("core")
    base = rhs[0, 0]
    up = upper_inverse[0, 0]
    low = lower_inverse[0, 0]
    width, nrhs = base.shape
    piece = width // ncol
    count = parents.shape[0]
    top = count // 2
    late = count - nz
    row = lax.axis_index(ROW)
    col = lax.axis_index(COL)
    panel = shape_of(width, nrhs)
    half_to_top = shape_of(top, piece // 2, nrhs)
    copies = shape_of(ny, piece, nrhs)
    across = shape_of(2 * ny, piece, nrhs)
    to_top = shape_of(top, piece, nrhs)
    to_late = shape_of(nz, piece, nrhs)

    sent = slot_call(
        turn_kernel, shape_of(ncol, piece, width), factor, pltpu.HBM,
        [
            pltpu.VMEM((ncol, piece, width), F32),
            pltpu.SemaphoreType.DMA((width // 128,)),
            pltpu.SemaphoreType.DMA((ncol,)),
        ],
    )
    below = slot_call(
        turn_whole_kernel, shape_of(width, width, kind=BF16), factor, pltpu.VMEM,
        [pltpu.SemaphoreType.DMA],
    )
    table = call(
        table_kernel, shape_of(HIGH + 1, count, nrhs),
        jnp.stack([row, col]).astype(jnp.int32), parents[None, :], parents[:, None],
        block_mask, scalars=1,
    )
    y0 = jnp.dot(up.astype(F32), base, precision=lax.Precision.HIGHEST)

    table, y0, base, up, low, below, sent = lax.optimization_barrier(
        (table, y0, base, up, low, below, sent)
    )
    slices = a2a(sent, COL)

    def total(line, first, got, shape, start=0, stop=ncol):
        body = functools.partial(sum_kernel, line, first, start, stop)
        return call(body, shape, table, got)

    def whole(half):
        return lax.all_gather(half, "core", tiled=True).reshape(width, nrhs)

    def spread(copied):
        return whole(a2a(copied, "y"))

    def spread_halves(copied):
        both = lax.all_gather(a2a(copied, BESIDE), "core", tiled=True)
        return both.reshape(ncol // ny, 2, ny, piece // 2, nrhs)

    out, own = call(leaf_kernel, (to_top, shape_of(width, width, kind=BF16)), slices, y0)
    got = total(FROM_LEAF, 0, a2a(out, HALF), across, start=ny)
    update = whole(a2a(got, ACROSS)[:ny])
    rest, out = call(one_kernel, (panel, half_to_top), update, base, up, own)
    got = total(FROM_ONE, top, a2a(out, HALF), half_to_top, start=ny)
    rest, out = call(
        two_kernel, (panel, to_late), spread_halves(got), rest, up, own
    )
    got = total(FROM_TWO, late, a2a(out, "z"), copies)
    y, out = call(three_kernel, (panel, to_late), spread(got), rest, up, low, own)
    got = total(FROM_THREE, late, a2a(out, "z"), copies)
    rest, out = call(two_back_kernel, (panel, half_to_top), spread(got), y, low, own)
    got = total(FROM_ABOVE, top, a2a(out, HALF), half_to_top, stop=ny)
    x, out = call(
        one_back_kernel, (panel, to_top), spread_halves(got), rest, low, below
    )
    got = total(TO_COLUMN, top, a2a(out, HALF), across, stop=ny)
    got = a2a(got, ACROSS)[ny:]
    got = lax.all_gather(got, "core")
    out = call(order_kernel, to_top, got)
    update = a2a(out, HALF).reshape(width, nrhs)
    return call(
        last_kernel, shape_of(1, 1, width, nrhs), table, update, y0, low, x
    )


def solution(mesh):
    grid = Mesh(mesh.devices.reshape(2, 2, 8, 8, 2), ("xh", "xl", "z", "y", "core"))
    placed = (
        P(ROW, None, COL, None, None, None),
        P(ROW, None, None, None),
        P(ROW, None, None, None),
        P(ROW, None, None, None),
        P(),
        P(),
    )
    return jax.shard_map(
        per_device,
        mesh=grid,
        in_specs=placed,
        out_specs=P(ROW, None, None, None),
        check_vma=False,
    )
```
